128 devices in a mesh: grp: 8 (over z, y_lo), blk: 16 (over x, y_hi, core).
Axes of the slice: x: 4, y: 4 (y_hi: 2, y_lo: 2; y = y_hi * 2 + y_lo), z: 4, core: 2. Of those that a mesh axis runs over, the one named last changes fastest.
Arguments:
- query: bfloat16 [16, 1024, 12288], P('blk', 'grp'), may hold values from -12 to 12
- latent: bfloat16 [16, 1024, 576], P('blk', 'grp'), may hold values from -12 to 12
- positions: int32 [16, 1024], P('blk'), may hold values from 0 to 255, as said below
- key_up: bfloat16 [512, 8192], P(None, 'grp'), may hold values from -0.25 to 0.25
- value_up: bfloat16 [512, 8192], P(None, 'grp'), may hold values from -0.25 to 0.25
- grad_out: bfloat16 [16, 1024, 8192], P('blk', None, 'grp'), may hold values from -6 to 6
Outputs:
- grad_query: bfloat16 [16, 1024, 12288], P('blk', None, 'grp')
- grad_latent: bfloat16 [16, 1024, 576], P('blk', 'grp')
The draws below stay inside these ranges and needn't reach their ends.
Inputs may be any that keep to these rules, and one draw needn't show every extreme that they name: positions[b, t] is the number of tokens that precede token t of group b in its document; documents are runs of consecutive tokens of the whole sequence, group after group; each has at most 256 tokens, and every one but the last of the sequence has at least 64.
All inputs are finite; a program needn't handle non-finite values.
Results may differ from the reference program's by a relative error of at most 0.02.
The reference program's roundings to bfloat16 on the way count: a program that leaves them out, or rounds other values in their place, can miss the bound.
Values may be sent and summed in bfloat16 or wider, within the bound.
A program may use at most 192 MiB of HBM per device.

```python
import math
import jax
import jax.numpy as jnp
from jax import lax

HEADS = 64
D_C = 512
D_R = 64
D_N = 128
D_V = 128
GROUP_TOK = 1024
NGROUPS = 16
TOKENS = 16384
DOC_MAX = 256


def draw_query(key, part):
    key = jax.random.fold_in(key, 1)
    head_width = D_N + D_R
    values = jnp.clip(jax.random.normal(key, (TOKENS, HEADS, head_width), jnp.float32), -6.0, 6.0)
    return values.reshape(NGROUPS, GROUP_TOK, HEADS * head_width).astype(jnp.bfloat16)


def draw_latent(key, part):
    key = jax.random.fold_in(key, 2)
    values = jnp.clip(jax.random.normal(key, (TOKENS, D_C + D_R), jnp.float32), -6.0, 6.0)
    return values.reshape(NGROUPS, GROUP_TOK, D_C + D_R).astype(jnp.bfloat16)


def draw_positions(key, part):
    key = jax.random.fold_in(key, 3)
    length_key, forced_key = jax.random.split(key)
    shortest = DOC_MAX // 4
    doc_count = TOKENS // shortest + 4
    doc_lengths = jax.random.randint(length_key, (doc_count,), shortest, DOC_MAX + 1)
    forced = jax.random.randint(forced_key, (), 0, NGROUPS - 1)
    doc_lengths = jnp.where(jnp.arange(doc_count) == forced, DOC_MAX, doc_lengths).astype(jnp.int32)
    starts = jnp.concatenate([jnp.zeros((1,), jnp.int32), jnp.cumsum(doc_lengths).astype(jnp.int32)])
    token_index = jnp.arange(TOKENS, dtype=jnp.int32)
    doc_begin = jnp.max(jnp.where(starts[:, None] <= token_index[None, :], starts[:, None], 0), axis=0)
    return (token_index - doc_begin).astype(jnp.int32).reshape(NGROUPS, GROUP_TOK)


def steps_of(stream_key, extent, cuts, least, high):
    gain = 1.0
    for dim, blocks in cuts:
        heights = jax.random.uniform(jax.random.fold_in(jax.random.fold_in(stream_key, 6), dim), (blocks,), jnp.float32, least / len(cuts), high / len(cuts))
        gain = gain * jnp.repeat(jnp.exp(heights), extent[dim] // blocks).reshape((-1,) + (1,) * (len(extent) - 1 - dim))
    return gain


def scatter_about(own_key, dims, scale, bound, cuts=(), kind=jnp.bfloat16):
    factor_of = steps_of(own_key, dims, cuts, -0.22, 0.18) if cuts else 1.0
    values = jax.random.normal(own_key, dims, jnp.float32) * scale * factor_of
    return jnp.minimum(jnp.maximum(values, -bound), bound).astype(kind)


def setup_inputs(seed: int = 0) -> dict:
    key_of = jax.random.split(jax.random.key(seed), 7)
    query = draw_query(jax.random.fold_in(key_of[6], 71), 0)
    latent = draw_latent(jax.random.fold_in(key_of[6], 71), 0)
    positions = draw_positions(jax.random.fold_in(key_of[6], 71), 0)
    key_up = scatter_about(key_of[3], (D_C, HEADS * D_N), D_C ** -0.5, 0.25, ((1, 8),))
    value_up = scatter_about(key_of[4], (D_C, HEADS * D_V), D_C ** -0.5, 0.25, ((1, 8),))
    grad_out = scatter_about(key_of[5], (NGROUPS, GROUP_TOK, HEADS * D_V), 1.0, 6.0, ((0, 16), (2, 8)))
    return dict(query=query, latent=latent, positions=positions, key_up=key_up, value_up=value_up, grad_out=grad_out)


rope_base = 10000.0
yarn_factor = 40.0
pretrain_context = 4096.0


def yarn_freqs(width):
    half_width = width // 2
    freq_index = jnp.arange(half_width, dtype=jnp.float32)
    extrapolated = rope_base ** (-2.0 * freq_index / width)
    lowest = max(math.floor(width * math.log(pretrain_context / (64.0 * math.pi)) / (2.0 * math.log(rope_base))), 0)
    highest = min(math.ceil(width * math.log(pretrain_context / (2.0 * math.pi)) / (2.0 * math.log(rope_base))), width - 1)
    ramp_up = jnp.clip((freq_index - lowest) / (highest - lowest), 0.0, 1.0)
    return extrapolated / yarn_factor * ramp_up + extrapolated * (1.0 - ramp_up)


def rotate(vectors, cos_table, sin_table, direction):
    half_width = vectors.shape[-1] // 2
    first_half = vectors[..., :half_width]
    second_half = vectors[..., half_width:]
    return jnp.concatenate([first_half * cos_table - direction * second_half * sin_table, second_half * cos_table + direction * first_half * sin_table], axis=-1)


def score_scaling():
    mscale = 0.1 * math.log(yarn_factor) + 1.0
    return (D_N + D_R) ** -0.5 * mscale * mscale


def attend_heads(query_nope, query_rot, grad_heads, keys_nope, values_heads, keys_rot, visible, scaling):
    scores = jnp.einsum("rhd,khd->hrk", query_nope.astype(jnp.float32), keys_nope.astype(jnp.float32))
    scores = (scores + jnp.einsum("rhd,kd->hrk", query_rot.astype(jnp.float32), keys_rot.astype(jnp.float32))) * scaling
    scores = jnp.where(visible[None], scores, -jnp.inf)
    top_score = jnp.max(scores, axis=-1, keepdims=True)
    weights = jnp.exp(scores - top_score)
    attention = weights / jnp.sum(weights, axis=-1, keepdims=True)
    attention_low = lax.optimization_barrier(attention.astype(jnp.bfloat16))
    grad_probs = jnp.einsum("rhd,khd->hrk", grad_heads.astype(jnp.float32), values_heads.astype(jnp.float32))
    delta_rows = jnp.sum(attention * grad_probs, axis=-1, keepdims=True)
    grad_scores = lax.optimization_barrier((attention * (grad_probs - delta_rows) * scaling).astype(jnp.bfloat16))
    grad_wide = grad_scores.astype(jnp.float32)
    grad_nope = jnp.einsum("hrk,khd->rhd", grad_wide, keys_nope.astype(jnp.float32))
    grad_rot = jnp.einsum("hrk,kd->rhd", grad_wide, keys_rot.astype(jnp.float32))
    keys_grad = jnp.einsum("hrk,rhd->khd", grad_wide, query_nope.astype(jnp.float32))
    values_grad = jnp.einsum("hrk,rhd->khd", attention_low.astype(jnp.float32), grad_heads.astype(jnp.float32))
    rot_grad = jnp.einsum("hrk,rhd->kd", grad_wide, query_rot.astype(jnp.float32))
    return grad_nope, grad_rot, keys_grad, values_grad, rot_grad


def reference(query, latent, positions, key_up, value_up, grad_out):
    group_tok = GROUP_TOK
    doc_max = DOC_MAX
    block_count = HEADS // 8
    scaling = score_scaling()
    angles = positions.astype(jnp.float32)[..., None] * yarn_freqs(D_R)
    cos_table = jnp.cos(angles)
    sin_table = jnp.sin(angles)
    key_rot = lax.optimization_barrier(rotate(latent[..., D_C:].astype(jnp.float32), cos_table, sin_table, 1.0).astype(jnp.bfloat16))
    compressed = latent[..., :D_C]
    earlier_c = jnp.concatenate([jnp.zeros_like(compressed[:1, group_tok - doc_max:]), compressed[:-1, group_tok - doc_max:]], axis=0)
    earlier_rot = jnp.concatenate([jnp.zeros_like(key_rot[:1, group_tok - doc_max:]), key_rot[:-1, group_tok - doc_max:]], axis=0)
    query_blocks = query.reshape(NGROUPS, group_tok, block_count, 8, D_N + D_R).transpose(0, 2, 1, 3, 4)
    grad_blocks = grad_out.reshape(NGROUPS, group_tok, block_count, 8, D_V).transpose(0, 2, 1, 3, 4)
    key_weights = key_up.reshape(D_C, block_count, 8 * D_N).transpose(1, 0, 2)
    value_weights = value_up.reshape(D_C, block_count, 8 * D_V).transpose(1, 0, 2)
    row_ids = jnp.arange(group_tok)
    col_ids = jnp.arange(doc_max + group_tok)
    key_rows = doc_max + group_tok

    def one_group(group_items):
        query_group, grad_group, cos_group, sin_group, pos_group, c_earlier, c_own, rot_earlier, rot_own = group_items
        both_c = jnp.concatenate([c_earlier, c_own], axis=0)
        both_rot = jnp.concatenate([rot_earlier, rot_own], axis=0)
        visible = (col_ids[None, :] >= doc_max + row_ids[:, None] - pos_group[:, None]) & (col_ids[None, :] <= doc_max + row_ids[:, None])
        cos_heads = cos_group[:, None, :]
        sin_heads = sin_group[:, None, :]

        def one_block(block_items):
            query_block, grad_block, key_weight, value_weight = block_items
            query_nope = query_block[..., :D_N]
            query_rot = lax.optimization_barrier(rotate(query_block[..., D_N:].astype(jnp.float32), cos_heads, sin_heads, 1.0).astype(jnp.bfloat16))
            keys_nope = lax.optimization_barrier(jnp.dot(both_c, key_weight, preferred_element_type=jnp.float32).astype(jnp.bfloat16))
            values_heads = lax.optimization_barrier(jnp.dot(both_c, value_weight, preferred_element_type=jnp.float32).astype(jnp.bfloat16))
            keys_nope = keys_nope.reshape(key_rows, 8, D_N)
            values_heads = values_heads.reshape(key_rows, 8, D_V)
            grad_nope, grad_rot, keys_grad, values_grad, rot_grad = attend_heads(query_nope, query_rot, grad_block, keys_nope, values_heads, both_rot, visible, scaling)
            key_low = lax.optimization_barrier(keys_grad.astype(jnp.bfloat16)).reshape(key_rows, 8 * D_N)
            value_low = lax.optimization_barrier(values_grad.astype(jnp.bfloat16)).reshape(key_rows, 8 * D_V)
            projected = jnp.dot(key_low, key_weight.T, preferred_element_type=jnp.float32)
            projected = projected + jnp.dot(value_low, value_weight.T, preferred_element_type=jnp.float32)
            grad_rot = rotate(grad_rot, cos_heads, sin_heads, -1.0)
            grad_query = jnp.concatenate([grad_nope, grad_rot], axis=-1).astype(jnp.bfloat16)
            return grad_query, projected, rot_grad

        grad_query, projected, rot_grad = lax.map(one_block, (query_group, grad_group, key_weights, value_weights))
        grad_query = grad_query.transpose(1, 0, 2, 3).reshape(group_tok, HEADS * (D_N + D_R))
        partial_value = jnp.concatenate([jnp.sum(projected, axis=0), jnp.sum(rot_grad, axis=0)], axis=1)
        return grad_query, partial_value

    grad_query, partial_value = lax.map(one_group, (query_blocks, grad_blocks, cos_table, sin_table, positions, earlier_c, compressed, earlier_rot, key_rot))
    later = jnp.concatenate([partial_value[1:, :doc_max], jnp.zeros((1, doc_max, D_C + D_R), jnp.float32)], axis=0)
    later = jnp.concatenate([jnp.zeros((NGROUPS, group_tok - doc_max, D_C + D_R), jnp.float32), later], axis=1)
    total = partial_value[:, doc_max:] + later
    rope_grad = rotate(total[..., D_C:], cos_table, sin_table, -1.0)
    grad_latent = jnp.concatenate([total[..., :D_C], rope_grad], axis=-1).astype(jnp.bfloat16)
    return grad_query, grad_latent
```

```python
import math

import jax
import jax.numpy as jnp
import numpy as np
from jax import lax
from jax.experimental import pallas as pl
from jax.experimental.pallas import tpu as pltpu
from jax.sharding import PartitionSpec as P

D_C = 512
D_R = 64
D_N = 128
D_V = 128
LANES = 128
BIG = -1e30

rope_base = 10000.0
yarn_factor = 40.0
pretrain_context = 4096.0

mscale = 0.1 * math.log(yarn_factor) + 1.0
SCALING = (D_N + D_R) ** (-0.5) * mscale * mscale

F32 = jnp.float32
BF16 = jnp.bfloat16
NT = (((1,), (1,)), ((), ()))
TN = (((0,), (0,)), ((), ()))
NN = (((1,), (0,)), ((), ()))


def dot(a, b, dims):
    return lax.dot_general(a, b, dims, preferred_element_type=F32)


def freqs_of(width):
    half_width = width // 2
    index = np.arange(half_width, dtype=np.float64)
    extrapolated = rope_base ** (-2.0 * index / width)
    span = 2.0 * math.log(rope_base)
    lowest = max(math.floor(width * math.log(pretrain_context / (64.0 * math.pi)) / span), 0)
    highest = min(math.ceil(width * math.log(pretrain_context / (2.0 * math.pi)) / span), width - 1)
    ramp = np.clip((index - lowest) / (highest - lowest), 0.0, 1.0)
    return (extrapolated / yarn_factor * ramp + extrapolated * (1.0 - ramp)).astype(np.float32)


def lane_of(rows):
    return lax.broadcasted_iota(jnp.int32, (rows, LANES), 1)


def swap_halves(m):
    lane = lane_of(m.shape[0])
    return jnp.where((lane & 32) == 0, pltpu.roll(m, 96, 1), pltpu.roll(m, 32, 1))


def from_behind(block, axis, distance):
    n = lax.axis_size(axis)
    route = [(i - distance, i) for i in range(n) if 0 <= i - distance < n]
    return lax.ppermute(block, axis, route)


def project_rows(first, rows, lat, key_up, value_up, kslot, krot, values):
    span = pl.ds(first, rows)
    low = lane_of(rows) < 64
    compressed = lat[span, :D_C]
    both = lat[span, D_C:].astype(F32)
    krot[span, :] = jnp.where(low, both, 0.0).astype(BF16)

    def pair(p, _):
        source = pl.ds(pl.multiple_of(p * 256, 256), 256)
        keys = dot(compressed, key_up[:, source], NN)
        values[span, source] = dot(compressed, value_up[:, source], NN).astype(BF16)
        turned = pltpu.roll(keys[:, 128:], 64, 1)
        kslot[span, pl.ds(pl.multiple_of(p * 384, 128), 128)] = keys[:, :128].astype(BF16)
        kslot[span, pl.ds(pl.multiple_of(p * 384 + 128, 128), 128)] = jnp.where(low, 0.0, turned).astype(BF16)
        kslot[span, pl.ds(pl.multiple_of(p * 384 + 256, 128), 128)] = jnp.where(low, turned, both).astype(BF16)
        return 0

    lax.fori_loop(0, key_up.shape[1] // 256, pair, 0)


def turn_queries(first, rows, qbuf, cos, sin):
    span = pl.ds(first, rows)
    low = lane_of(rows) < 64
    c, s = cos[span, :], sin[span, :]

    def pair(p, _):
        at1 = pl.ds(pl.multiple_of(p * 384 + 128, 128), 128)
        at2 = pl.ds(pl.multiple_of(p * 384 + 256, 128), 128)
        one, two = qbuf[span, at1].astype(F32), qbuf[span, at2].astype(F32)
        m = jnp.where(low, one, two)
        r = m * c + swap_halves(m) * s
        qbuf[span, at1] = jnp.where(low, r, one).astype(BF16)
        qbuf[span, at2] = jnp.where(low, two, r).astype(BF16)
        return 0

    lax.fori_loop(0, qbuf.shape[1] // 384, pair, 0)


def fill_bias(first, pos, bias):
    for half in range(2):
        p = pos[0:1, pl.ds(pl.multiple_of(first + half * 128, 128), 128)]
        c = lax.broadcasted_iota(jnp.int32, (384, 128), 0)
        r = lax.broadcasted_iota(jnp.int32, (384, 128), 1) + 256
        seen = (c <= r) & (c >= r - p)
        bias[half] = jnp.where(seen, 0.0, BIG)


def weigh(scores, dprob, bias):
    probs, grads = [], []
    for half in range(2):
        rows, cols = slice(128 * half, 128 * half + 384), slice(128 * half, 128 * half + 128)
        s = scores[rows, cols] + bias[half]
        d = dprob[rows, cols]
        top = jnp.max(s, axis=0, keepdims=True)
        e = jnp.exp((s - top) * SCALING)
        total = jnp.sum(e, axis=0, keepdims=True)
        delta = jnp.sum(e * d, axis=0, keepdims=True) / total
        prob = e * (1.0 / total)
        grad = (prob * (d - delta) * SCALING).astype(BF16)
        prob = prob.astype(BF16)
        none = jnp.zeros((128, 128), BF16)
        order = (lambda x: [x, none]) if half == 0 else (lambda x: [none, x])
        probs.append(jnp.concatenate(order(prob), axis=0))
        grads.append(jnp.concatenate(order(grad), axis=0))
    return jnp.concatenate(probs, axis=1), jnp.concatenate(grads, axis=1)


def attend(first, qbuf, gout, kslot, krot, values, bias, cos, sin, dq, dkacc, dvacc):
    qs, ks = pl.ds(first, 256), pl.ds(first, 512)

    def pair(p, _):
        s0 = pl.multiple_of(p * 384, 128)
        v0 = pl.multiple_of(p * 256, 256)
        q = qbuf[qs, pl.ds(s0, 384)]
        g = gout[qs, pl.ds(v0, 256)]
        k0 = jnp.concatenate([kslot[ks, pl.ds(s0, 128)], krot[ks, :]], axis=1)
        k1 = kslot[ks, pl.ds(pl.multiple_of(s0 + 128, 128), 256)]
        dqs, dks = [], []
        for odd, k in ((0, k0), (1, k1)):
            qh = q[:, 128 * odd : 128 * odd + 256]
            gh = g[:, 128 * odd : 128 * odd + 128]
            vh = values[ks, pl.ds(pl.multiple_of(v0 + 128 * odd, 128), 128)]
            scores = dot(k, qh, NT)
            dprob = dot(vh, gh, NT)
            prob, grad = weigh(scores, dprob, bias)
            dvacc[ks, pl.ds(pl.multiple_of(v0 + 128 * odd, 128), 128)] += dot(prob, gh, NN)
            dks.append(dot(grad, qh, NN))
            dqs.append(dot(grad, k, TN))
        low = lane_of(512) < 64
        dkacc[ks, pl.ds(s0, 128)] += dks[0][:, :128]
        dkacc[ks, pl.ds(pl.multiple_of(s0 + 128, 128), 128)] += jnp.where(low, dks[0][:, 128:], dks[1][:, :128])
        dkacc[ks, pl.ds(pl.multiple_of(s0 + 256, 128), 128)] += dks[1][:, 128:]
        low = lane_of(256) < 64
        one, two = dqs[0][:, 128:] + dqs[1][:, :128], dqs[1][:, 128:]
        m = jnp.where(low, one, two)
        r = m * cos[qs, :] - swap_halves(m) * sin[qs, :]
        dq[qs, pl.ds(s0, 128)] = dqs[0][:, :128].astype(BF16)
        dq[qs, pl.ds(pl.multiple_of(s0 + 128, 128), 128)] = jnp.where(low, r, one).astype(BF16)
        dq[qs, pl.ds(pl.multiple_of(s0 + 256, 128), 128)] = jnp.where(low, two, r).astype(BF16)
        return 0

    lax.fori_loop(0, qbuf.shape[1] // 384, pair, 0)


def gather_back(first, rows, key_up, value_up, dkacc, dvacc):
    span = pl.ds(first, rows)
    low = lane_of(rows) < 64
    total = jnp.zeros((rows, D_C), F32)
    turn = jnp.zeros((rows, LANES), F32)
    for p in range(key_up.shape[1] // 256):
        one = dkacc[span, 384 * p + 128 : 384 * p + 256]
        two = dkacc[span, 384 * p + 256 : 384 * p + 384]
        turn = turn + jnp.where(low, one, two)
        odd = pltpu.roll(jnp.where(low, two, one), 64, 1).astype(BF16)
        even = dkacc[span, 384 * p : 384 * p + 128].astype(BF16)
        cols = slice(256 * p, 256 * p + 256)
        total = total + dot(jnp.concatenate([even, odd], axis=1), key_up[:, cols], NT)
        total = total + dot(dvacc[span, cols].astype(BF16), value_up[:, cols], NT)
    return total, turn + pltpu.roll(turn, 64, 1)


def kernel(pos, qin, gout, lat, key_up, value_up, cos, sin, dq, part, qbuf, kslot, krot, values, bias, dkacc, dvacc):
    group_tok = qin.shape[0]
    qbuf[...] = qin[...]
    dkacc[...] = jnp.zeros_like(dkacc)
    dvacc[...] = jnp.zeros_like(dvacc)

    def prepare(j, _):
        project_rows(pl.multiple_of(j * 256, 256), 256, lat, key_up, value_up, kslot, krot, values)
        return 0

    lax.fori_loop(0, group_tok // 256 + 1, prepare, 0)

    def block(t, _):
        first = pl.multiple_of(t * 256, 256)
        turn_queries(first, 256, qbuf, cos, sin)
        fill_bias(first, pos, bias)
        attend(first, qbuf, gout, kslot, krot, values, bias, cos, sin, dq, dkacc, dvacc)
        return 0

    lax.fori_loop(0, group_tok // 256, block, 0)

    def finish(j, _):
        first = pl.multiple_of(j * 256, 256)
        total, turn = gather_back(first, 256, key_up, value_up, dkacc, dvacc)
        part[pl.ds(first, 256), :D_C] = total
        part[pl.ds(first, 256), D_C:] = turn
        return 0

    lax.fori_loop(0, group_tok // 256 + 1, finish, 0)


def per_device(query, latent, positions, key_up, value_up, grad_out):
    tok_dev = query.shape[1]
    group_tok = tok_dev * lax.axis_size("grp")
    key_rows = 256 + group_tok
    slots = query.shape[2] // lax.axis_size("grp")
    width = key_up.shape[1]
    freq = jnp.asarray(np.tile(freqs_of(D_R), 4))
    sign = jnp.asarray(np.where(np.arange(LANES) % 64 < 32, -1.0, 1.0).astype(np.float32))
    angles = positions[0].astype(F32)[:, None] * freq[None, :]
    cos, sin = jnp.cos(angles), jnp.sin(angles) * sign[None, :]
    own = lax.axis_index("grp") * tok_dev
    own_cos = lax.dynamic_slice_in_dim(cos, own, tok_dev, 0)[:, :D_R]
    own_sin = lax.dynamic_slice_in_dim(sin, own, tok_dev, 0)[:, :D_R]

    def turned(u, way):
        return u * own_cos + way * jnp.concatenate([u[:, 32:], u[:, :32]], axis=1) * own_sin

    rot = turned(latent[0, :, D_C:].astype(F32), 1.0).astype(BF16)
    piece = jnp.concatenate([latent[0, :, :D_C], rot, rot], axis=1)
    rows = lax.all_gather(piece, "grp", axis=0, tiled=True)
    query_heads = lax.all_to_all(query[0], "grp", split_axis=1, concat_axis=0, tiled=True)
    lat = jnp.concatenate([from_behind(rows[group_tok - 256 :], "blk", 1), rows], axis=0)
    grad_query, part = pl.pallas_call(
        kernel,
        out_shape=(
            jax.ShapeDtypeStruct((group_tok, slots), BF16),
            jax.ShapeDtypeStruct((key_rows, D_C + LANES), F32),
        ),
        in_specs=[pl.BlockSpec(memory_space=pltpu.VMEM)] * 8,
        out_specs=(pl.BlockSpec(memory_space=pltpu.VMEM),) * 2,
        scratch_shapes=[
            pltpu.VMEM((group_tok, slots), BF16),
            pltpu.VMEM((key_rows, slots), BF16),
            pltpu.VMEM((key_rows, LANES), BF16),
            pltpu.VMEM((key_rows, width), BF16),
            pltpu.VMEM((2, 384, 128), F32),
            pltpu.VMEM((key_rows, slots), F32),
            pltpu.VMEM((key_rows, width), F32),
        ],
        compiler_params=pltpu.CompilerParams(vmem_limit_bytes=60 * 1024 * 1024),
    )(positions, query_heads, grad_out[0], lat, key_up, value_up, cos, sin)
    part = part[:, : D_C + D_R]
    own_part = part[256:]
    returned = from_behind(part[:256], "blk", -1)
    own_part = jnp.concatenate([own_part[: group_tok - 256], own_part[group_tok - 256 :] + returned], axis=0)
    summed = lax.psum_scatter(own_part, "grp", scatter_dimension=0, tiled=True)
    grad_latent = jnp.concatenate([summed[:, :D_C], turned(summed[:, D_C:], -1.0)], axis=1).astype(BF16)
    return (grad_query[None], grad_latent[None])


def solution(mesh):
    placed = (
        P("blk", "grp", None),
        P("blk", "grp", None),
        P("blk", None),
        P(None, "grp"),
        P(None, "grp"),
        P("blk", None, "grp"),
    )
    return jax.shard_map(
        per_device,
        mesh=mesh,
        in_specs=placed,
        out_specs=(P("blk", None, "grp"), P("blk", "grp", None)),
        check_vma=False,
    )
```

```python
import math

import jax
import jax.numpy as jnp
import numpy as np
from jax import lax
from jax.experimental import pallas as pl
from jax.experimental.pallas import tpu as pltpu
from jax.sharding import PartitionSpec as P

D_C = 512
D_R = 64
D_N = 128
D_V = 128
LANES = 128
BIG = -1e30

rope_base = 10000.0
yarn_factor = 40.0
pretrain_context = 4096.0

mscale = 0.1 * math.log(yarn_factor) + 1.0
SCALING = (D_N + D_R) ** (-0.5) * mscale * mscale

F32 = jnp.float32
BF16 = jnp.bfloat16
NT = (((1,), (1,)), ((), ()))
TN = (((0,), (0,)), ((), ()))
NN = (((1,), (0,)), ((), ()))


def dot(a, b, dims):
    return lax.dot_general(a, b, dims, preferred_element_type=F32)


def freqs_of(width):
    half_width = width // 2
    index = np.arange(half_width, dtype=np.float64)
    extrapolated = rope_base ** (-2.0 * index / width)
    span = 2.0 * math.log(rope_base)
    lowest = max(math.floor(width * math.log(pretrain_context / (64.0 * math.pi)) / span), 0)
    highest = min(math.ceil(width * math.log(pretrain_context / (2.0 * math.pi)) / span), width - 1)
    ramp = np.clip((index - lowest) / (highest - lowest), 0.0, 1.0)
    return (extrapolated / yarn_factor * ramp + extrapolated * (1.0 - ramp)).astype(np.float32)


def lane_of(rows):
    return lax.broadcasted_iota(jnp.int32, (rows, LANES), 1)


def swap_halves(m):
    lane = lane_of(m.shape[0])
    return jnp.where((lane & 32) == 0, pltpu.roll(m, 96, 1), pltpu.roll(m, 32, 1))


def fill_tables(first, pos, freq, cos, sin):
    p = pos[0:1, pl.ds(pl.multiple_of(first, 128), 128)].astype(F32)
    angles = jnp.broadcast_to(p, (128, 128)).T * freq[0:1, :]
    span = pl.ds(first, 128)
    cos[span, :] = jnp.cos(angles)
    s = jnp.sin(angles)
    sin[span, :] = jnp.where((lane_of(128) & 32) == 0, -s, s)


def project_rows(first, rows, lat, key_up, value_up, kslot, krot, values):
    span = pl.ds(first, rows)
    low = lane_of(rows) < 64
    compressed = lat[span, :D_C]
    both = lat[span, D_C:].astype(F32)
    krot[span, :] = jnp.where(low, both, 0.0).astype(BF16)

    def pair(p, _):
        source = pl.ds(pl.multiple_of(p * 256, 256), 256)
        keys = dot(compressed, key_up[:, source], NN)
        values[span, source] = dot(compressed, value_up[:, source], NN).astype(BF16)
        turned = pltpu.roll(keys[:, 128:], 64, 1)
        kslot[span, pl.ds(pl.multiple_of(p * 384, 128), 128)] = keys[:, :128].astype(BF16)
        kslot[span, pl.ds(pl.multiple_of(p * 384 + 128, 128), 128)] = jnp.where(low, 0.0, turned).astype(BF16)
        kslot[span, pl.ds(pl.multiple_of(p * 384 + 256, 128), 128)] = jnp.where(low, turned, both).astype(BF16)
        return 0

    lax.fori_loop(0, key_up.shape[1] // 256, pair, 0)


def turn_queries(first, rows, qbuf, cos, sin):
    span = pl.ds(first, rows)
    low = lane_of(rows) < 64
    c, s = cos[span, :], sin[span, :]

    def pair(p, _):
        at1 = pl.ds(pl.multiple_of(p * 384 + 128, 128), 128)
        at2 = pl.ds(pl.multiple_of(p * 384 + 256, 128), 128)
        one, two = qbuf[span, at1].astype(F32), qbuf[span, at2].astype(F32)
        m = jnp.where(low, one, two)
        r = m * c + swap_halves(m) * s
        qbuf[span, at1] = jnp.where(low, r, one).astype(BF16)
        qbuf[span, at2] = jnp.where(low, two, r).astype(BF16)
        return 0

    lax.fori_loop(0, qbuf.shape[1] // 384, pair, 0)


def fill_bias(first, pos, bias):
    for half in range(2):
        p = pos[0:1, pl.ds(pl.multiple_of(first + half * 128, 128), 128)]
        c = lax.broadcasted_iota(jnp.int32, (384, 128), 0)
        r = lax.broadcasted_iota(jnp.int32, (384, 128), 1) + 256
        seen = (c <= r) & (c >= r - p)
        bias[half] = jnp.where(seen, 0.0, BIG)


def weigh(scores, dprob, bias):
    probs, grads = [], []
    for half in range(2):
        rows, cols = slice(128 * half, 128 * half + 384), slice(128 * half, 128 * half + 128)
        s = scores[rows, cols] + bias[half]
        d = dprob[rows, cols]
        top = jnp.max(s, axis=0, keepdims=True)
        e = jnp.exp((s - top) * SCALING)
        total = jnp.sum(e, axis=0, keepdims=True)
        delta = jnp.sum(e * d, axis=0, keepdims=True) / total
        prob = e * (1.0 / total)
        grad = (prob * (d - delta) * SCALING).astype(BF16)
        prob = prob.astype(BF16)
        none = jnp.zeros((128, 128), BF16)
        order = (lambda x: [x, none]) if half == 0 else (lambda x: [none, x])
        probs.append(jnp.concatenate(order(prob), axis=0))
        grads.append(jnp.concatenate(order(grad), axis=0))
    return jnp.concatenate(probs, axis=1), jnp.concatenate(grads, axis=1)


def attend(first, qbuf, gout, kslot, krot, values, bias, cos, sin, dq, dkacc, dvacc):
    qs, ks = pl.ds(first, 256), pl.ds(first, 512)

    def pair(p, _):
        s0 = pl.multiple_of(p * 384, 128)
        v0 = pl.multiple_of(p * 256, 256)
        q = qbuf[qs, pl.ds(s0, 384)]
        g = gout[qs, pl.ds(v0, 256)]
        k0 = jnp.concatenate([kslot[ks, pl.ds(s0, 128)], krot[ks, :]], axis=1)
        k1 = kslot[ks, pl.ds(pl.multiple_of(s0 + 128, 128), 256)]
        dqs, dks = [], []
        for odd, k in ((0, k0), (1, k1)):
            qh = q[:, 128 * odd : 128 * odd + 256]
            gh = g[:, 128 * odd : 128 * odd + 128]
            vh = values[ks, pl.ds(pl.multiple_of(v0 + 128 * odd, 128), 128)]
            scores = dot(k, qh, NT)
            dprob = dot(vh, gh, NT)
            prob, grad = weigh(scores, dprob, bias)
            dvacc[ks, pl.ds(pl.multiple_of(v0 + 128 * odd, 128), 128)] += dot(prob, gh, NN)
            dks.append(dot(grad, qh, NN))
            dqs.append(dot(grad, k, TN))
        low = lane_of(512) < 64
        dkacc[ks, pl.ds(s0, 128)] += dks[0][:, :128]
        dkacc[ks, pl.ds(pl.multiple_of(s0 + 128, 128), 128)] += jnp.where(low, dks[0][:, 128:], dks[1][:, :128])
        dkacc[ks, pl.ds(pl.multiple_of(s0 + 256, 128), 128)] += dks[1][:, 128:]
        low = lane_of(256) < 64
        one, two = dqs[0][:, 128:] + dqs[1][:, :128], dqs[1][:, 128:]
        m = jnp.where(low, one, two)
        r = m * cos[qs, :] - swap_halves(m) * sin[qs, :]
        dq[qs, pl.ds(s0, 128)] = dqs[0][:, :128].astype(BF16)
        dq[qs, pl.ds(pl.multiple_of(s0 + 128, 128), 128)] = jnp.where(low, r, one).astype(BF16)
        dq[qs, pl.ds(pl.multiple_of(s0 + 256, 128), 128)] = jnp.where(low, two, r).astype(BF16)
        return 0

    lax.fori_loop(0, qbuf.shape[1] // 384, pair, 0)


def gather_back(first, rows, key_up, value_up, dkacc, dvacc):
    span = pl.ds(first, rows)
    low = lane_of(rows) < 64
    total = jnp.zeros((rows, D_C), F32)
    turn = jnp.zeros((rows, LANES), F32)
    for p in range(key_up.shape[1] // 256):
        one = dkacc[span, 384 * p + 128 : 384 * p + 256]
        two = dkacc[span, 384 * p + 256 : 384 * p + 384]
        turn = turn + jnp.where(low, one, two)
        odd = pltpu.roll(jnp.where(low, two, one), 64, 1).astype(BF16)
        even = dkacc[span, 384 * p : 384 * p + 128].astype(BF16)
        cols = slice(256 * p, 256 * p + 256)
        total = total + dot(jnp.concatenate([even, odd], axis=1), key_up[:, cols], NT)
        total = total + dot(dvacc[span, cols].astype(BF16), value_up[:, cols], NT)
    return total, turn + pltpu.roll(turn, 64, 1)


STEPS = ((0, 1), (1, 0), (1, 1), (3, 0), (3, 1), (2, 0), (2, 1))


def kernel(
    query, gout_hbm, lat_in, pos, key_hbm, value_hbm, freq, dq_hbm, glat,
    qbuf, lat, gout, key_up, value_up, cos, sin, kslot, krot, values, bias, dkacc, dvacc, dq, sbuf, own, rbuf, hbuf,
    load_sem, store_sem, lat_send, lat_recv, q_send, q_recv, g_send, g_recv, h_send, h_recv,
):
    g, b = lax.axis_index("grp"), lax.axis_index("blk")
    nb = lax.axis_size("blk")
    z, y = g // 2, g % 2
    slots = qbuf.shape[1]
    group_tok = qbuf.shape[0]
    ahead, behind = (b + 1) % nb, (b + nb - 1) % nb

    def peer(step, way=1):
        return ((z + 4 + way * step[0]) % 4) * 2 + (y + step[1]) % 2

    def remote(src, dst, send, recv, to_g=None, to_b=None):
        return pltpu.make_async_remote_copy(
            src_ref=src,
            dst_ref=dst,
            send_sem=send,
            recv_sem=recv,
            device_id=(g if to_g is None else to_g, b if to_b is None else to_b),
            device_id_type=pl.DeviceIdType.MESH,
        )

    loads = [
        pltpu.make_async_copy(key_hbm, key_up, load_sem.at[0]),
        pltpu.make_async_copy(value_hbm, value_up, load_sem.at[1]),
        pltpu.make_async_copy(
            query.at[:, pl.ds(pl.multiple_of(g * slots, 128), slots)],
            qbuf.at[pl.ds(pl.multiple_of(g * 128, 128), 128), :],
            load_sem.at[2],
        ),
        pltpu.make_async_copy(gout_hbm, gout, load_sem.at[3]),
    ]
    for load in loads:
        load.start()

    barrier = pltpu.get_barrier_semaphore()
    for step in STEPS:
        pl.semaphore_signal(barrier, inc=1, device_id=(peer(step), b), device_id_type=pl.DeviceIdType.MESH)
    for other in (ahead, behind):
        pl.semaphore_signal(barrier, inc=1, device_id=(g, other), device_id_type=pl.DeviceIdType.MESH)

    my = pl.multiple_of(g * 128, 128)
    mine = pl.ds(my, 128)
    fill_tables(my, pos, freq, cos, sin)
    raw = lat_in[:, D_C:].astype(F32)
    raw = jnp.concatenate([raw, raw], axis=1)
    turned = (raw * cos[mine, :] + swap_halves(raw) * sin[mine, :]).astype(BF16)
    my_rows = pl.ds(pl.multiple_of(256 + g * 128, 128), 128)
    lat[my_rows, :D_C] = lat_in[:, :D_C]
    lat[my_rows, D_C:] = turned

    pl.semaphore_wait(barrier, 9)
    lat_copies = [
        remote(lat.at[my_rows, :], lat.at[my_rows, :], lat_send.at[i], lat_recv.at[i], to_g=peer(step))
        for i, step in enumerate(STEPS)
    ]
    for copy in lat_copies:
        copy.start()
    q_copies = [
        remote(
            query.at[:, pl.ds(pl.multiple_of(peer(step) * slots, 128), slots)],
            qbuf.at[mine, :],
            q_send.at[i],
            q_recv.at[i],
            to_g=peer(step),
        )
        for i, step in enumerate(STEPS)
    ]
    for copy in q_copies:
        copy.start()

    dkacc[...] = jnp.zeros_like(dkacc)
    dvacc[...] = jnp.zeros_like(dvacc)

    def table(t, _):
        fill_tables(pl.multiple_of(t * 128, 128), pos, freq, cos, sin)
        return 0

    lax.fori_loop(0, group_tok // 128, table, 0)

    for copy in lat_copies:
        copy.wait_recv()
    halo = remote(lat.at[pl.ds(group_tok, 256), :], lat.at[pl.ds(0, 256), :], h_send.at[0], h_recv.at[0], to_b=ahead)
    halo.start()
    loads[0].wait()
    loads[1].wait()

    def prepare(j, _):
        project_rows(pl.multiple_of(j * 256, 256), 256, lat, key_up, value_up, kslot, krot, values)
        return 0

    lax.fori_loop(1, group_tok // 256 + 1, prepare, 0)
    halo.wait_recv()
    prepare(0, 0)
    loads[2].wait()
    loads[3].wait()

    stores = []
    for i, (way, arrivals) in enumerate(((0, (0,)), (-1, (1, 2)), (1, (3, 4)), (2, (5, 6)))):
        for a in arrivals:
            q_copies[a].wait_recv()
        first = pl.multiple_of(((z + 4 + way) % 4) * 256, 256)
        turn_queries(first, 256, qbuf, cos, sin)
        fill_bias(first, pos, bias)
        attend(first, qbuf, gout, kslot, krot, values, bias, cos, sin, dq, dkacc, dvacc)
        store = pltpu.make_async_copy(dq.at[pl.ds(first, 256), :], dq_hbm.at[pl.ds(first, 256), :], store_sem.at[i])
        store.start()
        stores.append(store)

    total, turn = gather_back(0, 256, key_up, value_up, dkacc, dvacc)
    sbuf[0:256, :D_C] = total.astype(BF16)
    sbuf[0:256, D_C:] = turn.astype(BF16)
    back = remote(sbuf.at[0:256, :], hbuf, h_send.at[1], h_recv.at[1], to_b=behind)
    back.start()

    g_copies = []
    for way in (2, 1, 3, 0):
        block = (z + way) % 4
        first = pl.multiple_of(256 + block * 256, 256)
        total, turn = gather_back(first, 256, key_up, value_up, dkacc, dvacc)
        own[:, :D_C] = total
        own[:, D_C:] = turn

        @pl.when(block == 3)
        def _():
            back.wait_recv()
            own[...] += hbuf[...].astype(F32)

        if way:
            sbuf[pl.ds(first, 256), :] = own[...].astype(BF16)
        else:
            first = pl.multiple_of(first + (1 - y) * 128, 128)
            sbuf[pl.ds(first, 128), :] = own[pl.ds(pl.multiple_of((1 - y) * 128, 128), 128), :].astype(BF16)
        for i, step in enumerate(STEPS):
            if step[0] == way:
                rows = pl.ds(pl.multiple_of(256 + peer(step) * 128, 128), 128)
                copy = remote(sbuf.at[rows, :], rbuf.at[i], g_send.at[i], g_recv.at[i], to_g=peer(step))
                copy.start()
                g_copies.append(copy)

    total = own[pl.ds(pl.multiple_of(y * 128, 128), 128), :]
    for copy in g_copies:
        copy.wait_recv()
    for i in range(len(STEPS)):
        total = total + rbuf[i].astype(F32)
    turn = total[:, D_C:]
    turn = turn * cos[mine, :] - swap_halves(turn) * sin[mine, :]
    glat[:, :D_C] = total[:, :D_C].astype(BF16)
    glat[:, D_C:] = turn[:, :D_R].astype(BF16)

    for copy in lat_copies + q_copies + g_copies + [halo, back]:
        copy.wait_send()
    for store in stores:
        store.wait()


def per_device(query, latent, positions, key_up, value_up, grad_out):
    tok_dev = query.shape[1]
    group_tok = tok_dev * lax.axis_size("grp")
    key_rows = 256 + group_tok
    slots = query.shape[2] // lax.axis_size("grp")
    width = key_up.shape[1]
    wide = D_C + LANES
    freq = jnp.asarray(np.tile(freqs_of(D_R), 4)[None])
    hbm, vmem = pl.BlockSpec(memory_space=pl.ANY), pl.BlockSpec(memory_space=pltpu.VMEM)
    dma = pltpu.SemaphoreType.DMA
    grad_query, grad_latent = pl.pallas_call(
        kernel,
        out_shape=(
            jax.ShapeDtypeStruct((group_tok, slots), BF16),
            jax.ShapeDtypeStruct((tok_dev, D_C + D_R), BF16),
        ),
        in_specs=[hbm, hbm, vmem, vmem, hbm, hbm, vmem],
        out_specs=(hbm, vmem),
        scratch_shapes=[
            pltpu.VMEM((group_tok, slots), BF16),
            pltpu.VMEM((key_rows, wide), BF16),
            pltpu.VMEM((group_tok, width), BF16),
            pltpu.VMEM((D_C, width), BF16),
            pltpu.VMEM((D_C, width), BF16),
            pltpu.VMEM((group_tok, LANES), F32),
            pltpu.VMEM((group_tok, LANES), F32),
            pltpu.VMEM((key_rows, slots), BF16),
            pltpu.VMEM((key_rows, LANES), BF16),
            pltpu.VMEM((key_rows, width), BF16),
            pltpu.VMEM((2, 384, 128), F32),
            pltpu.VMEM((key_rows, slots), F32),
            pltpu.VMEM((key_rows, width), F32),
            pltpu.VMEM((group_tok, slots), BF16),
            pltpu.VMEM((key_rows, wide), BF16),
            pltpu.VMEM((256, wide), F32),
            pltpu.VMEM((7, tok_dev, wide), BF16),
            pltpu.VMEM((256, wide), BF16),
            dma((4,)),
            dma((4,)),
            dma((7,)),
            dma((7,)),
            dma((7,)),
            dma((7,)),
            dma((7,)),
            dma((7,)),
            dma((2,)),
            dma((2,)),
        ],
        compiler_params=pltpu.CompilerParams(
            vmem_limit_bytes=60 * 1024 * 1024, collective_id=0, has_side_effects=True
        ),
    )(query[0], grad_out[0], latent[0], positions, key_up, value_up, freq)
    return (grad_query[None], grad_latent[None])


def solution(mesh):
    placed = (
        P("blk", "grp", None),
        P("blk", "grp", None),
        P("blk", None),
        P(None, "grp"),
        P(None, "grp"),
        P("blk", None, "grp"),
    )
    return jax.shard_map(
        per_device,
        mesh=mesh,
        in_specs=placed,
        out_specs=(P("blk", None, "grp"), P("blk", "grp", None)),
        check_vma=False,
    )
```

```python
import math

import jax
import jax.numpy as jnp
import numpy as np
from jax import lax
from jax.experimental import pallas as pl
from jax.experimental.pallas import tpu as pltpu
from jax.sharding import PartitionSpec as P

D_C = 512
D_R = 64
D_N = 128
D_V = 128
LANES = 128
BIG = -1e30

rope_base = 10000.0
yarn_factor = 40.0
pretrain_context = 4096.0

mscale = 0.1 * math.log(yarn_factor) + 1.0
SCALING = (D_N + D_R) ** (-0.5) * mscale * mscale

F32 = jnp.float32
BF16 = jnp.bfloat16
NT = (((1,), (1,)), ((), ()))
TN = (((0,), (0,)), ((), ()))
NN = (((1,), (0,)), ((), ()))


def dot(a, b, dims):
    return lax.dot_general(a, b, dims, preferred_element_type=F32)


def freqs_of(width):
    half_width = width // 2
    index = np.arange(half_width, dtype=np.float64)
    extrapolated = rope_base ** (-2.0 * index / width)
    span = 2.0 * math.log(rope_base)
    lowest = max(math.floor(width * math.log(pretrain_context / (64.0 * math.pi)) / span), 0)
    highest = min(math.ceil(width * math.log(pretrain_context / (2.0 * math.pi)) / span), width - 1)
    ramp = np.clip((index - lowest) / (highest - lowest), 0.0, 1.0)
    return (extrapolated / yarn_factor * ramp + extrapolated * (1.0 - ramp)).astype(np.float32)


def lane_of(rows):
    return lax.broadcasted_iota(jnp.int32, (rows, LANES), 1)


def swap_halves(m):
    lane = lane_of(m.shape[0])
    return jnp.where((lane & 32) == 0, pltpu.roll(m, 96, 1), pltpu.roll(m, 32, 1))


def fill_tables(first, pos, freq, cos, sin):
    p = pos[0:1, pl.ds(pl.multiple_of(first, 128), 128)].astype(F32)
    angles = jnp.broadcast_to(p, (128, 128)).T * freq[0:1, :]
    span = pl.ds(first, 128)
    cos[span, :] = jnp.cos(angles)
    s = jnp.sin(angles)
    sin[span, :] = jnp.where((lane_of(128) & 32) == 0, -s, s)


def project_rows(first, rows, lat, key_up, value_up, kslot, krot, values):
    span = pl.ds(first, rows)
    low = lane_of(rows) < 64
    compressed = lat[span, :D_C]
    both = lat[span, D_C:].astype(F32)
    krot[span, :] = jnp.where(low, both, 0.0).astype(BF16)

    def pair(p, _):
        source = pl.ds(pl.multiple_of(p * 256, 256), 256)
        keys = dot(compressed, key_up[:, source], NN)
        values[span, source] = dot(compressed, value_up[:, source], NN).astype(BF16)
        turned = pltpu.roll(keys[:, 128:], 64, 1)
        kslot[span, pl.ds(pl.multiple_of(p * 384, 128), 128)] = keys[:, :128].astype(BF16)
        kslot[span, pl.ds(pl.multiple_of(p * 384 + 128, 128), 128)] = jnp.where(low, 0.0, turned).astype(BF16)
        kslot[span, pl.ds(pl.multiple_of(p * 384 + 256, 128), 128)] = jnp.where(low, turned, both).astype(BF16)
        return 0

    lax.fori_loop(0, key_up.shape[1] // 256, pair, 0)


def turn_queries(first, rows, qbuf, cos, sin):
    span = pl.ds(first, rows)
    low = lane_of(rows) < 64
    c, s = cos[span, :], sin[span, :]

    def pair(p, _):
        at1 = pl.ds(pl.multiple_of(p * 384 + 128, 128), 128)
        at2 = pl.ds(pl.multiple_of(p * 384 + 256, 128), 128)
        one, two = qbuf[span, at1].astype(F32), qbuf[span, at2].astype(F32)
        m = jnp.where(low, one, two)
        r = m * c + swap_halves(m) * s
        qbuf[span, at1] = jnp.where(low, r, one).astype(BF16)
        qbuf[span, at2] = jnp.where(low, two, r).astype(BF16)
        return 0

    lax.fori_loop(0, qbuf.shape[1] // 384, pair, 0)


def fill_bias(first, pos, bias):
    for half in range(2):
        p = pos[0:1, pl.ds(pl.multiple_of(first + half * 128, 128), 128)]
        c = lax.broadcasted_iota(jnp.int32, (384, 128), 0)
        r = lax.broadcasted_iota(jnp.int32, (384, 128), 1) + 256
        seen = (c <= r) & (c >= r - p)
        bias[half] = jnp.where(seen, 0.0, BIG)


def weigh(scores, dprob, bias):
    probs, grads = [], []
    for half in range(2):
        rows, cols = slice(128 * half, 128 * half + 384), slice(128 * half, 128 * half + 128)
        s = scores[rows, cols] + bias[half]
        d = dprob[rows, cols]
        top = jnp.max(s, axis=0, keepdims=True)
        e = jnp.exp((s - top) * SCALING)
        total = jnp.sum(e, axis=0, keepdims=True)
        delta = jnp.sum(e * d, axis=0, keepdims=True) / total
        prob = e * (1.0 / total)
        grad = (prob * (d - delta) * SCALING).astype(BF16)
        prob = prob.astype(BF16)
        none = jnp.zeros((128, 128), BF16)
        order = (lambda x: [x, none]) if half == 0 else (lambda x: [none, x])
        probs.append(jnp.concatenate(order(prob), axis=0))
        grads.append(jnp.concatenate(order(grad), axis=0))
    return jnp.concatenate(probs, axis=1), jnp.concatenate(grads, axis=1)


def attend(first, qbuf, gout, kslot, krot, values, bias, cos, sin, dq, dkacc, dvacc):
    qs, ks = pl.ds(first, 256), pl.ds(first, 512)

    def pair(p, _):
        s0 = pl.multiple_of(p * 384, 128)
        v0 = pl.multiple_of(p * 256, 256)
        q = qbuf[qs, pl.ds(s0, 384)]
        g = gout[qs, pl.ds(v0, 256)]
        k0 = jnp.concatenate([kslot[ks, pl.ds(s0, 128)], krot[ks, :]], axis=1)
        k1 = kslot[ks, pl.ds(pl.multiple_of(s0 + 128, 128), 256)]
        dqs, dks = [], []
        for odd, k in ((0, k0), (1, k1)):
            qh = q[:, 128 * odd : 128 * odd + 256]
            gh = g[:, 128 * odd : 128 * odd + 128]
            vh = values[ks, pl.ds(pl.multiple_of(v0 + 128 * odd, 128), 128)]
            scores = dot(k, qh, NT)
            dprob = dot(vh, gh, NT)
            prob, grad = weigh(scores, dprob, bias)
            dvacc[ks, pl.ds(pl.multiple_of(v0 + 128 * odd, 128), 128)] += dot(prob, gh, NN)
            dks.append(dot(grad, qh, NN))
            dqs.append(dot(grad, k, TN))
        low = lane_of(512) < 64
        dkacc[ks, pl.ds(s0, 128)] += dks[0][:, :128]
        dkacc[ks, pl.ds(pl.multiple_of(s0 + 128, 128), 128)] += jnp.where(low, dks[0][:, 128:], dks[1][:, :128])
        dkacc[ks, pl.ds(pl.multiple_of(s0 + 256, 128), 128)] += dks[1][:, 128:]
        low = lane_of(256) < 64
        one, two = dqs[0][:, 128:] + dqs[1][:, :128], dqs[1][:, 128:]
        m = jnp.where(low, one, two)
        r = m * cos[qs, :] - swap_halves(m) * sin[qs, :]
        dq[qs, pl.ds(s0, 128)] = dqs[0][:, :128].astype(BF16)
        dq[qs, pl.ds(pl.multiple_of(s0 + 128, 128), 128)] = jnp.where(low, r, one).astype(BF16)
        dq[qs, pl.ds(pl.multiple_of(s0 + 256, 128), 128)] = jnp.where(low, two, r).astype(BF16)
        return 0

    lax.fori_loop(0, qbuf.shape[1] // 384, pair, 0)


def gather_back(first, rows, key_up, value_up, dkacc, dvacc):
    span = pl.ds(first, rows)
    low = lane_of(rows) < 64
    total = jnp.zeros((rows, D_C), F32)
    turn = jnp.zeros((rows, LANES), F32)
    for p in range(key_up.shape[1] // 256):
        one = dkacc[span, 384 * p + 128 : 384 * p + 256]
        two = dkacc[span, 384 * p + 256 : 384 * p + 384]
        turn = turn + jnp.where(low, one, two)
        odd = pltpu.roll(jnp.where(low, two, one), 64, 1).astype(BF16)
        even = dkacc[span, 384 * p : 384 * p + 128].astype(BF16)
        cols = slice(256 * p, 256 * p + 256)
        total = total + dot(jnp.concatenate([even, odd], axis=1), key_up[:, cols], NT)
        total = total + dot(dvacc[span, cols].astype(BF16), value_up[:, cols], NT)
    return total, turn + pltpu.roll(turn, 64, 1)


STEPS = ((0, 1), (1, 0), (1, 1), (3, 0), (3, 1), (2, 0), (2, 1))


def kernel(
    query, gout_hbm, lat_in, pos, key_hbm, value_hbm, freq, dq_hbm, glat,
    qbuf, lat, gout, key_up, value_up, cos, sin, kslot, krot, values, bias, dkacc, dvacc, dq, sbuf, own, rbuf, hbuf,
    load_sem, store_sem, lat_send, lat_recv, q_send, q_recv, g_send, g_recv, h_send, h_recv,
):
    g, b = lax.axis_index("grp"), lax.axis_index("blk")
    nb = lax.axis_size("blk")
    z, y = g // 2, g % 2
    slots = qbuf.shape[1]
    group_tok = qbuf.shape[0]
    ahead, behind = (b + 1) % nb, (b + nb - 1) % nb

    def peer(step):
        return ((z + step[0]) % 4) * 2 + (y + step[1]) % 2

    def remote(src, dst, send, recv, to_g=None, to_b=None):
        return pltpu.make_async_remote_copy(
            src_ref=src,
            dst_ref=dst,
            send_sem=send,
            recv_sem=recv,
            device_id=(g if to_g is None else to_g, b if to_b is None else to_b),
            device_id_type=pl.DeviceIdType.MESH,
        )

    loads = [
        pltpu.make_async_copy(key_hbm, key_up, load_sem.at[0]),
        pltpu.make_async_copy(value_hbm, value_up, load_sem.at[1]),
        pltpu.make_async_copy(
            query.at[:, pl.ds(pl.multiple_of(g * slots, 128), slots)],
            qbuf.at[pl.ds(pl.multiple_of(g * 128, 128), 128), :],
            load_sem.at[2],
        ),
        pltpu.make_async_copy(gout_hbm, gout, load_sem.at[3]),
    ]

    barrier = pltpu.get_barrier_semaphore()
    for step in STEPS:
        pl.semaphore_signal(barrier, inc=1, device_id=(peer(step), b), device_id_type=pl.DeviceIdType.MESH)
    for other in (ahead, behind):
        pl.semaphore_signal(barrier, inc=1, device_id=(g, other), device_id_type=pl.DeviceIdType.MESH)

    my = pl.multiple_of(g * 128, 128)
    mine = pl.ds(my, 128)
    fill_tables(my, pos, freq, cos, sin)

    def rows_of(gg):
        return pl.ds(pl.multiple_of(256 + gg * 128, 128), 128)

    raw = lat_in[D_C:, :].astype(F32)
    raw = jnp.concatenate([raw, raw], axis=0).T
    turned = (raw * cos[mine, :] + swap_halves(raw) * sin[mine, :]).astype(BF16)
    lat[rows_of(g), :D_C] = lat_in[:D_C, :].astype(F32).T.astype(BF16)
    lat[rows_of(g), D_C:] = turned

    pl.semaphore_wait(barrier, 9)

    def lat_copy(i, of_g, to_g):
        return remote(lat.at[rows_of(of_g), :], lat.at[rows_of(of_g), :], lat_send.at[i], lat_recv.at[i], to_g=to_g)

    mate = z * 2 + 1 - y
    first_copies = [lat_copy(0, g, mate)] + [
        lat_copy(1 + i, g, peer((dz, 0))) for i, dz in enumerate((1, 3, 2))
    ]
    for copy in first_copies:
        copy.start()
    q_copies = {
        step: remote(
            query.at[:, pl.ds(pl.multiple_of(peer(step) * slots, 128), slots)],
            qbuf.at[mine, :],
            q_send.at[i],
            q_recv.at[i],
            to_g=peer(step),
        )
        for i, step in enumerate(STEPS)
    }
    q_copies[(0, 1)].start()
    for load in loads:
        load.start()
    first_copies[0].wait_recv()
    second_copies = [lat_copy(4 + i, mate, peer((dz, 0))) for i, dz in enumerate((1, 3, 2))]
    for copy in second_copies:
        copy.start()
    lat_copies = first_copies + second_copies

    dkacc[...] = jnp.zeros_like(dkacc)
    dvacc[...] = jnp.zeros_like(dvacc)

    def table(t, _):
        fill_tables(pl.multiple_of(t * 128, 128), pos, freq, cos, sin)
        return 0

    lax.fori_loop(0, group_tok // 128, table, 0)

    for copy in lat_copies:
        copy.wait_send()
    for copy in lat_copies[1:]:
        copy.wait_recv()
    halo = remote(lat.at[pl.ds(group_tok, 256), :], lat.at[pl.ds(0, 256), :], h_send.at[0], h_recv.at[0], to_b=ahead)
    halo.start()
    for step in ((1, 0), (3, 0), (1, 1), (3, 1)):
        q_copies[step].start()
    loads[0].wait()
    loads[1].wait()

    project_rows(256, group_tok, lat, key_up, value_up, kslot, krot, values)
    loads[2].wait()
    loads[3].wait()
    halo.wait_recv()
    project_rows(0, 256, lat, key_up, value_up, kslot, krot, values)

    back = remote(sbuf.at[0:256, :], hbuf, h_send.at[1], h_recv.at[1], to_b=behind)
    g_copies = []

    def return_halo():
        total, turn = gather_back(0, 256, key_up, value_up, dkacc, dvacc)
        sbuf[0:256, :D_C] = total.astype(BF16)
        sbuf[0:256, D_C:] = turn.astype(BF16)
        back.start()

    def send_back(way):
        block = (z + way) % 4
        first = pl.multiple_of(256 + block * 256, 256)
        total, turn = gather_back(first, 256, key_up, value_up, dkacc, dvacc)
        if way:
            sbuf[pl.ds(first, 256), :D_C] = total.astype(BF16)
            sbuf[pl.ds(first, 256), D_C:] = turn.astype(BF16)
        else:
            own[:, :D_C] = total
            own[:, D_C:] = turn

        @pl.when(block == 3)
        def _():
            back.wait_recv()
            if way:
                sbuf[pl.ds(first, 256), :] = (sbuf[pl.ds(first, 256), :].astype(F32) + hbuf[...].astype(F32)).astype(BF16)
            else:
                own[...] += hbuf[...].astype(F32)

        if not way:
            row = pl.multiple_of((1 - y) * 128, 128)
            sbuf[pl.ds(pl.multiple_of(first + row, 128), 128), :] = own[pl.ds(row, 128), :].astype(BF16)
        for i, step in enumerate(STEPS):
            if step[0] == way:
                copy = remote(sbuf.at[rows_of(peer(step)), :], rbuf.at[i], g_send.at[i], g_recv.at[i], to_g=peer(step))
                copy.start()
                g_copies.append(copy)

    stores = []
    for i, way in enumerate((0, 3, 1, 2)):
        block = (z + way) % 4
        for dy in (0, 1):
            step = ((4 - way) % 4, dy)
            if step in q_copies:
                q_copies[step].wait_recv()
        first = pl.multiple_of(block * 256, 256)
        turn_queries(first, 256, qbuf, cos, sin)
        fill_bias(first, pos, bias)
        attend(first, qbuf, gout, kslot, krot, values, bias, cos, sin, dq, dkacc, dvacc)
        store = pltpu.make_async_copy(dq.at[pl.ds(first, 256), :], dq_hbm.at[pl.ds(first, 256), :], store_sem.at[i])
        store.start()
        stores.append(store)
        if i == 0:
            q_copies[(2, 0)].start()
            q_copies[(2, 1)].start()
        pl.when(block == 0)(return_halo)
        if i == 1:
            send_back(3)
        if i == 2:
            send_back(0)
        if i == 3:
            send_back(2)
            send_back(1)

    total = own[pl.ds(pl.multiple_of(y * 128, 128), 128), :]
    for copy in g_copies:
        copy.wait_recv()
    for i in range(len(STEPS)):
        total = total + rbuf[i].astype(F32)
    turn = total[:, D_C:]
    turn = turn * cos[mine, :] - swap_halves(turn) * sin[mine, :]
    glat[:D_C, :] = total[:, :D_C].T.astype(BF16)
    glat[D_C:, :] = turn.T[:D_R, :].astype(BF16)

    for copy in list(q_copies.values()) + g_copies + [halo, back]:
        copy.wait_send()
    for store in stores:
        store.wait()


def per_device(query, latent, positions, key_up, value_up, grad_out):
    tok_dev = query.shape[1]
    group_tok = tok_dev * lax.axis_size("grp")
    key_rows = 256 + group_tok
    slots = query.shape[2] // lax.axis_size("grp")
    width = key_up.shape[1]
    wide = D_C + LANES
    freq = jnp.asarray(np.tile(freqs_of(D_R), 4)[None])
    hbm, vmem = pl.BlockSpec(memory_space=pl.ANY), pl.BlockSpec(memory_space=pltpu.VMEM)
    dma = pltpu.SemaphoreType.DMA
    grad_query, grad_latent = pl.pallas_call(
        kernel,
        out_shape=(
            jax.ShapeDtypeStruct((group_tok, slots), BF16),
            jax.ShapeDtypeStruct((D_C + D_R, tok_dev), BF16),
        ),
        in_specs=[hbm, hbm, vmem, vmem, hbm, hbm, vmem],
        out_specs=(hbm, vmem),
        scratch_shapes=[
            pltpu.VMEM((group_tok, slots), BF16),
            pltpu.VMEM((key_rows, wide), BF16),
            pltpu.VMEM((group_tok, width), BF16),
            pltpu.VMEM((D_C, width), BF16),
            pltpu.VMEM((D_C, width), BF16),
            pltpu.VMEM((group_tok, LANES), F32),
            pltpu.VMEM((group_tok, LANES), F32),
            pltpu.VMEM((key_rows, slots), BF16),
            pltpu.VMEM((key_rows, LANES), BF16),
            pltpu.VMEM((key_rows, width), BF16),
            pltpu.VMEM((2, 384, 128), F32),
            pltpu.VMEM((key_rows, slots), F32),
            pltpu.VMEM((key_rows, width), F32),
            pltpu.VMEM((group_tok, slots), BF16),
            pltpu.VMEM((key_rows, wide), BF16),
            pltpu.VMEM((256, wide), F32),
            pltpu.VMEM((7, tok_dev, wide), BF16),
            pltpu.VMEM((256, wide), BF16),
            dma((4,)),
            dma((4,)),
            dma((7,)),
            dma((7,)),
            dma((7,)),
            dma((7,)),
            dma((7,)),
            dma((7,)),
            dma((2,)),
            dma((2,)),
        ],
        compiler_params=pltpu.CompilerParams(
            vmem_limit_bytes=60 * 1024 * 1024, collective_id=0, has_side_effects=True
        ),
    )(query[0], grad_out[0], latent[0].T, positions, key_up, value_up, freq)
    return (grad_query[None], grad_latent.T[None])


def solution(mesh):
    placed = (
        P("blk", "grp", None),
        P("blk", "grp", None),
        P("blk", None),
        P(None, "grp"),
        P(None, "grp"),
        P("blk", None, "grp"),
    )
    return jax.shard_map(
        per_device,
        mesh=mesh,
        in_specs=placed,
        out_specs=(P("blk", None, "grp"), P("blk", "grp", None)),
        check_vma=False,
    )
```

```python
import math

import jax
import jax.numpy as jnp
import numpy as np
from jax import lax
from jax.experimental import pallas as pl
from jax.experimental.pallas import tpu as pltpu
from jax.sharding import PartitionSpec as P

D_C = 512
D_R = 64
D_N = 128
D_V = 128
LANES = 128
BIG = -1e30

rope_base = 10000.0
yarn_factor = 40.0
pretrain_context = 4096.0

mscale = 0.1 * math.log(yarn_factor) + 1.0
SCALING = (D_N + D_R) ** (-0.5) * mscale * mscale

F32 = jnp.float32
BF16 = jnp.bfloat16
NT = (((1,), (1,)), ((), ()))
TN = (((0,), (0,)), ((), ()))
NN = (((1,), (0,)), ((), ()))


def dot(a, b, dims):
    return lax.dot_general(a, b, dims, preferred_element_type=F32)


def freqs_of(width):
    half_width = width // 2
    index = np.arange(half_width, dtype=np.float64)
    extrapolated = rope_base ** (-2.0 * index / width)
    span = 2.0 * math.log(rope_base)
    lowest = max(math.floor(width * math.log(pretrain_context / (64.0 * math.pi)) / span), 0)
    highest = min(math.ceil(width * math.log(pretrain_context / (2.0 * math.pi)) / span), width - 1)
    ramp = np.clip((index - lowest) / (highest - lowest), 0.0, 1.0)
    return (extrapolated / yarn_factor * ramp + extrapolated * (1.0 - ramp)).astype(np.float32)


def lane_of(rows):
    return lax.broadcasted_iota(jnp.int32, (rows, LANES), 1)


def swap_halves(m):
    lane = lane_of(m.shape[0])
    return jnp.where((lane & 32) == 0, pltpu.roll(m, 96, 1), pltpu.roll(m, 32, 1))


def fill_tables(first, pos, freq, cos, sin):
    p = pos[0:1, pl.ds(pl.multiple_of(first, 128), 128)].astype(F32)
    angles = jnp.broadcast_to(p, (128, 128)).T * freq[0:1, :]
    span = pl.ds(first, 128)
    cos[span, :] = jnp.cos(angles)
    s = jnp.sin(angles)
    sin[span, :] = jnp.where((lane_of(128) & 32) == 0, -s, s)


def project_rows(first, rows, lat, key_up, value_up, kslot, krot, values):
    span = pl.ds(first, rows)
    low = lane_of(rows) < 64
    compressed = lat[span, :D_C]
    both = lat[span, D_C:].astype(F32)
    krot[span, :] = jnp.where(low, both, 0.0).astype(BF16)

    def pair(p, _):
        source = pl.ds(pl.multiple_of(p * 256, 256), 256)
        keys = dot(compressed, key_up[:, source], NN)
        values[span, source] = dot(compressed, value_up[:, source], NN).astype(BF16)
        turned = pltpu.roll(keys[:, 128:], 64, 1)
        kslot[span, pl.ds(pl.multiple_of(p * 384, 128), 128)] = keys[:, :128].astype(BF16)
        kslot[span, pl.ds(pl.multiple_of(p * 384 + 128, 128), 128)] = jnp.where(low, 0.0, turned).astype(BF16)
        kslot[span, pl.ds(pl.multiple_of(p * 384 + 256, 128), 128)] = jnp.where(low, turned, both).astype(BF16)
        return 0

    lax.fori_loop(0, key_up.shape[1] // 256, pair, 0)


def turn_queries(first, rows, pairs, qbuf, cos, sin):
    span = pl.ds(first, rows)
    low = lane_of(rows) < 64
    c, s = cos[span, :], sin[span, :]

    def pair(p, _):
        at1 = pl.ds(pl.multiple_of(p * 384 + 128, 128), 128)
        at2 = pl.ds(pl.multiple_of(p * 384 + 256, 128), 128)
        one, two = qbuf[span, at1].astype(F32), qbuf[span, at2].astype(F32)
        m = jnp.where(low, one, two)
        r = m * c + swap_halves(m) * s
        qbuf[span, at1] = jnp.where(low, r, one).astype(BF16)
        qbuf[span, at2] = jnp.where(low, two, r).astype(BF16)
        return 0

    lax.fori_loop(*pairs, pair, 0)


def fill_bias(first, pos, bias):
    for half in range(2):
        p = pos[0:1, pl.ds(pl.multiple_of(first + half * 128, 128), 128)]
        c = lax.broadcasted_iota(jnp.int32, (384, 128), 0)
        r = lax.broadcasted_iota(jnp.int32, (384, 128), 1) + 256
        seen = (c <= r) & (c >= r - p)
        bias[half] = jnp.where(seen, 0.0, BIG)


def weigh(scores, dprob, bias):
    probs, grads = [], []
    for half in range(2):
        rows, cols = slice(128 * half, 128 * half + 384), slice(128 * half, 128 * half + 128)
        s = scores[rows, cols] + bias[half]
        d = dprob[rows, cols]
        top = jnp.max(s, axis=0, keepdims=True)
        e = jnp.exp((s - top) * SCALING)
        total = jnp.sum(e, axis=0, keepdims=True)
        delta = jnp.sum(e * d, axis=0, keepdims=True) / total
        prob = e * (1.0 / total)
        grad = (prob * (d - delta) * SCALING).astype(BF16)
        prob = prob.astype(BF16)
        none = jnp.zeros((128, 128), BF16)
        order = (lambda x: [x, none]) if half == 0 else (lambda x: [none, x])
        probs.append(jnp.concatenate(order(prob), axis=0))
        grads.append(jnp.concatenate(order(grad), axis=0))
    return jnp.concatenate(probs, axis=1), jnp.concatenate(grads, axis=1)


def attend(first, pairs, qbuf, gout, kslot, krot, values, bias, cos, sin, dq, dkacc, dvacc):
    qs, ks = pl.ds(first, 256), pl.ds(first, 512)

    def pair(p, _):
        s0 = pl.multiple_of(p * 384, 128)
        v0 = pl.multiple_of(p * 256, 256)
        q = qbuf[qs, pl.ds(s0, 384)]
        g = gout[qs, pl.ds(v0, 256)]
        k0 = jnp.concatenate([kslot[ks, pl.ds(s0, 128)], krot[ks, :]], axis=1)
        k1 = kslot[ks, pl.ds(pl.multiple_of(s0 + 128, 128), 256)]
        dqs, dks = [], []
        for odd, k in ((0, k0), (1, k1)):
            qh = q[:, 128 * odd : 128 * odd + 256]
            gh = g[:, 128 * odd : 128 * odd + 128]
            vh = values[ks, pl.ds(pl.multiple_of(v0 + 128 * odd, 128), 128)]
            scores = dot(k, qh, NT)
            dprob = dot(vh, gh, NT)
            prob, grad = weigh(scores, dprob, bias)
            dvacc[ks, pl.ds(pl.multiple_of(v0 + 128 * odd, 128), 128)] += dot(prob, gh, NN)
            dks.append(dot(grad, qh, NN))
            dqs.append(dot(grad, k, TN))
        low = lane_of(512) < 64
        dkacc[ks, pl.ds(s0, 128)] += dks[0][:, :128]
        dkacc[ks, pl.ds(pl.multiple_of(s0 + 128, 128), 128)] += jnp.where(low, dks[0][:, 128:], dks[1][:, :128])
        dkacc[ks, pl.ds(pl.multiple_of(s0 + 256, 128), 128)] += dks[1][:, 128:]
        low = lane_of(256) < 64
        one, two = dqs[0][:, 128:] + dqs[1][:, :128], dqs[1][:, 128:]
        m = jnp.where(low, one, two)
        r = m * cos[qs, :] - swap_halves(m) * sin[qs, :]
        dq[qs, pl.ds(s0, 128)] = dqs[0][:, :128].astype(BF16)
        dq[qs, pl.ds(pl.multiple_of(s0 + 128, 128), 128)] = jnp.where(low, r, one).astype(BF16)
        dq[qs, pl.ds(pl.multiple_of(s0 + 256, 128), 128)] = jnp.where(low, two, r).astype(BF16)
        return 0

    lax.fori_loop(*pairs, pair, 0)


def gather_back(first, rows, key_up, value_up, dkacc, dvacc):
    span = pl.ds(first, rows)
    low = lane_of(rows) < 64
    total = jnp.zeros((rows, D_C), F32)
    turn = jnp.zeros((rows, LANES), F32)
    for p in range(key_up.shape[1] // 256):
        one = dkacc[span, 384 * p + 128 : 384 * p + 256]
        two = dkacc[span, 384 * p + 256 : 384 * p + 384]
        turn = turn + jnp.where(low, one, two)
        odd = pltpu.roll(jnp.where(low, two, one), 64, 1).astype(BF16)
        even = dkacc[span, 384 * p : 384 * p + 128].astype(BF16)
        cols = slice(256 * p, 256 * p + 256)
        total = total + dot(jnp.concatenate([even, odd], axis=1), key_up[:, cols], NT)
        total = total + dot(dvacc[span, cols].astype(BF16), value_up[:, cols], NT)
    return total, turn + pltpu.roll(turn, 64, 1)


STEPS = ((0, 1), (1, 0), (1, 1), (3, 0), (3, 1), (2, 0), (2, 1))


def kernel(
    query, gout_hbm, lat_in, pos, key_hbm, value_hbm, freq, dq_hbm, glat,
    qbuf, lat, gout, key_up, value_up, cos, sin, kslot, krot, values, bias, dkacc, dvacc, dq, sbuf, own, keep, mbuf, rbuf, hbuf,
    load_sem, store_sem, lat_send, lat_recv, q_send, q_recv, m_send, m_recv, g_send, g_recv, h_send, h_recv,
):
    g, b = lax.axis_index("grp"), lax.axis_index("blk")
    nb = lax.axis_size("blk")
    z, y = g // 2, g % 2
    slots = qbuf.shape[1]
    group_tok = qbuf.shape[0]
    ahead, behind = (b + 1) % nb, (b + nb - 1) % nb

    def peer(step):
        return ((z + step[0]) % 4) * 2 + (y + step[1]) % 2

    def remote(src, dst, send, recv, to_g=None, to_b=None):
        return pltpu.make_async_remote_copy(
            src_ref=src,
            dst_ref=dst,
            send_sem=send,
            recv_sem=recv,
            device_id=(g if to_g is None else to_g, b if to_b is None else to_b),
            device_id_type=pl.DeviceIdType.MESH,
        )

    loads = [
        pltpu.make_async_copy(key_hbm, key_up, load_sem.at[0]),
        pltpu.make_async_copy(value_hbm, value_up, load_sem.at[1]),
        pltpu.make_async_copy(
            query.at[:, pl.ds(pl.multiple_of(g * slots, 128), slots)],
            qbuf.at[pl.ds(pl.multiple_of(g * 128, 128), 128), :],
            load_sem.at[2],
        ),
        pltpu.make_async_copy(gout_hbm, gout, load_sem.at[3]),
    ]

    barrier = pltpu.get_barrier_semaphore()
    for step in STEPS:
        pl.semaphore_signal(barrier, inc=1, device_id=(peer(step), b), device_id_type=pl.DeviceIdType.MESH)
    for other in (ahead, behind):
        pl.semaphore_signal(barrier, inc=1, device_id=(g, other), device_id_type=pl.DeviceIdType.MESH)

    my = pl.multiple_of(g * 128, 128)
    mine = pl.ds(my, 128)
    fill_tables(my, pos, freq, cos, sin)

    def rows_of(gg):
        return pl.ds(pl.multiple_of(256 + gg * 128, 128), 128)

    raw = lat_in[D_C:, :].astype(F32)
    raw = jnp.concatenate([raw, raw], axis=0).T
    turned = (raw * cos[mine, :] + swap_halves(raw) * sin[mine, :]).astype(BF16)
    lat[rows_of(g), :D_C] = lat_in[:D_C, :].astype(F32).T.astype(BF16)
    lat[rows_of(g), D_C:] = turned

    pl.semaphore_wait(barrier, 9)

    def lat_copy(i, of_g, to_g, begin=0, rows=128):
        span = pl.ds(pl.multiple_of(256 + of_g * 128 + begin, 64), rows)
        return remote(lat.at[span, :], lat.at[span, :], lat_send.at[i], lat_recv.at[i], to_g=to_g)

    mate = z * 2 + 1 - y
    hops = (1, 3, 2)
    lat_copies = [lat_copy(0, g, mate)] + [lat_copy(1 + i, g, peer((dz, 0))) for i, dz in enumerate(hops)]
    for copy in lat_copies:
        copy.start()
    for load in loads:
        load.start()
    lat_copies[0].wait_recv()
    for i, dz in enumerate(hops):
        copy = lat_copy(4 + i, mate, peer((dz, 0)), 64, 64)
        copy.start()
        lat_copies.append(copy)
    for i, dz in enumerate(hops):
        lat_copies[1 + i].wait_recv()
        copy = lat_copy(7 + i, ((z + 4 - dz) % 4) * 2 + y, mate, 0, 64)
        copy.start()
        lat_copies.append(copy)

    half = slots // 2
    q_copies = {}
    for dz, dy in STEPS:
        for part in (0, 1) if dz == 2 else (None,):
            n = len(q_copies)
            begin, count = (0, slots) if part is None else (part * half, half)
            q_copies[(dz, dy, part)] = remote(
                query.at[:, pl.ds(pl.multiple_of(peer((dz, dy)) * slots + begin, 128), count)],
                qbuf.at[mine, begin : begin + count],
                q_send.at[n],
                q_recv.at[n],
                to_g=peer((dz, dy)),
            )
    q_copies[(0, 1, None)].start()

    dkacc[...] = jnp.zeros_like(dkacc)
    dvacc[...] = jnp.zeros_like(dvacc)

    def table(t, _):
        fill_tables(pl.multiple_of(t * 128, 128), pos, freq, cos, sin)
        return 0

    lax.fori_loop(0, group_tok // 128, table, 0)

    for copy in lat_copies:
        copy.wait_send()
    q_copies[(1, 0, None)].start()
    q_copies[(3, 0, None)].start()
    for copy in lat_copies[4:]:
        copy.wait_recv()
    halo = remote(lat.at[pl.ds(group_tok, 256), :], lat.at[pl.ds(0, 256), :], h_send.at[0], h_recv.at[0], to_b=ahead)
    halo.start()
    q_copies[(1, 1, None)].start()
    q_copies[(3, 1, None)].start()
    loads[0].wait()
    loads[1].wait()

    project_rows(256, group_tok, lat, key_up, value_up, kslot, krot, values)
    loads[2].wait()
    loads[3].wait()
    halo.wait_recv()
    project_rows(0, 256, lat, key_up, value_up, kslot, krot, values)

    back = remote(sbuf.at[0:256, :], hbuf, h_send.at[1], h_recv.at[1], to_b=behind)
    def return_halo():
        total, turn = gather_back(0, 256, key_up, value_up, dkacc, dvacc)
        sbuf[0:256, :D_C] = total.astype(BF16)
        sbuf[0:256, D_C:] = turn.astype(BF16)
        back.start()

    mate_copies = {}

    def send_mate(way):
        block = (z + way) % 4
        total, turn = gather_back(pl.multiple_of(256 + block * 256, 256), 256, key_up, value_up, dkacc, dvacc)
        own[:, :D_C] = total
        own[:, D_C:] = turn

        @pl.when(block == 3)
        def _():
            back.wait_recv()
            own[...] += hbuf[...].astype(F32)

        keep[way] = own[pl.ds(pl.multiple_of(y * 128, 128), 128), :]
        span = rows_of(block * 2 + 1 - y)
        sbuf[span, :] = own[pl.ds(pl.multiple_of((1 - y) * 128, 128), 128), :].astype(BF16)
        mate_copies[way] = remote(sbuf.at[span, :], mbuf.at[way], m_send.at[way], m_recv.at[way], to_g=mate)
        mate_copies[way].start()

    z_copies = []

    def send_on(way):
        span = rows_of(((z + way) % 4) * 2 + y)
        mate_copies[way].wait_recv()
        sbuf[span, :] = (keep[way] + mbuf[way].astype(F32)).astype(BF16)
        copy = remote(sbuf.at[span, :], rbuf.at[way - 1], g_send.at[way - 1], g_recv.at[way - 1], to_g=peer((way, 0)))
        copy.start()
        z_copies.append(copy)

    stores = []
    for i, way in enumerate((0, 3, 1, 2)):
        block = (z + way) % 4
        first = pl.multiple_of(block * 256, 256)
        for part in (0, 1) if way == 2 else (None,):
            for dy in (0, 1):
                if way or dy:
                    q_copies[((4 - way) % 4, dy, part)].wait_recv()
            if part == 1:
                send_on(3)
            pairs = (0, slots // 384) if part is None else (part * slots // 768, (part + 1) * slots // 768)
            turn_queries(first, 256, pairs, qbuf, cos, sin)
            if not part:
                fill_bias(first, pos, bias)
            attend(first, pairs, qbuf, gout, kslot, krot, values, bias, cos, sin, dq, dkacc, dvacc)
        store = pltpu.make_async_copy(dq.at[pl.ds(first, 256), :], dq_hbm.at[pl.ds(first, 256), :], store_sem.at[i])
        store.start()
        stores.append(store)
        if i < 2:
            q_copies[(2, 0, i)].start()
            q_copies[(2, 1, i)].start()
        pl.when(block == 0)(return_halo)
        if i == 1:
            send_mate(3)
        if i == 2:
            send_mate(0)
        if i == 3:
            send_mate(2)
            send_mate(1)
            send_on(2)
            send_on(1)

    mate_copies[0].wait_recv()
    total = keep[0] + mbuf[0].astype(F32)
    for copy in z_copies:
        copy.wait_recv()
    for i in range(3):
        total = total + rbuf[i].astype(F32)
    turn = total[:, D_C:]
    turn = turn * cos[mine, :] - swap_halves(turn) * sin[mine, :]
    glat[:D_C, :] = total[:, :D_C].T.astype(BF16)
    glat[D_C:, :] = turn.T[:D_R, :].astype(BF16)

    for copy in [*q_copies.values(), *mate_copies.values(), *z_copies, halo, back]:
        copy.wait_send()
    for store in stores:
        store.wait()


def per_device(query, latent, positions, key_up, value_up, grad_out):
    tok_dev = query.shape[1]
    group_tok = tok_dev * lax.axis_size("grp")
    key_rows = 256 + group_tok
    slots = query.shape[2] // lax.axis_size("grp")
    width = key_up.shape[1]
    wide = D_C + LANES
    freq = jnp.asarray(np.tile(freqs_of(D_R), 4)[None])
    hbm, vmem = pl.BlockSpec(memory_space=pl.ANY), pl.BlockSpec(memory_space=pltpu.VMEM)
    dma = pltpu.SemaphoreType.DMA
    grad_query, grad_latent = pl.pallas_call(
        kernel,
        out_shape=(
            jax.ShapeDtypeStruct((group_tok, slots), BF16),
            jax.ShapeDtypeStruct((D_C + D_R, tok_dev), BF16),
        ),
        in_specs=[hbm, hbm, vmem, vmem, hbm, hbm, vmem],
        out_specs=(hbm, vmem),
        scratch_shapes=[
            pltpu.VMEM((group_tok, slots), BF16),
            pltpu.VMEM((key_rows, wide), BF16),
            pltpu.VMEM((group_tok, width), BF16),
            pltpu.VMEM((D_C, width), BF16),
            pltpu.VMEM((D_C, width), BF16),
            pltpu.VMEM((group_tok, LANES), F32),
            pltpu.VMEM((group_tok, LANES), F32),
            pltpu.VMEM((key_rows, slots), BF16),
            pltpu.VMEM((key_rows, LANES), BF16),
            pltpu.VMEM((key_rows, width), BF16),
            pltpu.VMEM((2, 384, 128), F32),
            pltpu.VMEM((key_rows, slots), F32),
            pltpu.VMEM((key_rows, width), F32),
            pltpu.VMEM((group_tok, slots), BF16),
            pltpu.VMEM((key_rows, wide), BF16),
            pltpu.VMEM((256, wide), F32),
            pltpu.VMEM((4, tok_dev, wide), F32),
            pltpu.VMEM((4, tok_dev, wide), BF16),
            pltpu.VMEM((3, tok_dev, wide), BF16),
            pltpu.VMEM((256, wide), BF16),
            dma((4,)),
            dma((4,)),
            dma((10,)),
            dma((10,)),
            dma((9,)),
            dma((9,)),
            dma((4,)),
            dma((4,)),
            dma((3,)),
            dma((3,)),
            dma((2,)),
            dma((2,)),
        ],
        compiler_params=pltpu.CompilerParams(
            vmem_limit_bytes=60 * 1024 * 1024, collective_id=0, has_side_effects=True
        ),
    )(query[0], grad_out[0], latent[0].T, positions, key_up, value_up, freq)
    return (grad_query[None], grad_latent.T[None])


def solution(mesh):
    placed = (
        P("blk", "grp", None),
        P("blk", "grp", None),
        P("blk", None),
        P(None, "grp"),
        P(None, "grp"),
        P("blk", None, "grp"),
    )
    return jax.shard_map(
        per_device,
        mesh=mesh,
        in_specs=placed,
        out_specs=(P("blk", None, "grp"), P("blk", "grp", None)),
        check_vma=False,
    )
```

```python
import math

import jax
import jax.numpy as jnp
import numpy as np
from jax import lax
from jax.experimental import pallas as pl
from jax.experimental.pallas import tpu as pltpu
from jax.sharding import PartitionSpec as P

D_C = 512
D_R = 64
D_N = 128
D_V = 128
LANES = 128
BIG = -1e30

rope_base = 10000.0
yarn_factor = 40.0
pretrain_context = 4096.0

mscale = 0.1 * math.log(yarn_factor) + 1.0
SCALING = (D_N + D_R) ** (-0.5) * mscale * mscale

F32 = jnp.float32
BF16 = jnp.bfloat16
NT = (((1,), (1,)), ((), ()))
TN = (((0,), (0,)), ((), ()))
NN = (((1,), (0,)), ((), ()))


def dot(a, b, dims):
    return lax.dot_general(a, b, dims, preferred_element_type=F32)


def freqs_of(width):
    half_width = width // 2
    index = np.arange(half_width, dtype=np.float64)
    extrapolated = rope_base ** (-2.0 * index / width)
    span = 2.0 * math.log(rope_base)
    lowest = max(math.floor(width * math.log(pretrain_context / (64.0 * math.pi)) / span), 0)
    highest = min(math.ceil(width * math.log(pretrain_context / (2.0 * math.pi)) / span), width - 1)
    ramp = np.clip((index - lowest) / (highest - lowest), 0.0, 1.0)
    return (extrapolated / yarn_factor * ramp + extrapolated * (1.0 - ramp)).astype(np.float32)


def lane_of(rows):
    return lax.broadcasted_iota(jnp.int32, (rows, LANES), 1)


def swap_halves(m):
    lane = lane_of(m.shape[0])
    return jnp.where((lane & 32) == 0, pltpu.roll(m, 96, 1), pltpu.roll(m, 32, 1))


def fill_tables(first, pos, freq, cos, sin):
    p = pos[0:1, pl.ds(pl.multiple_of(first, 128), 128)].astype(F32)
    angles = jnp.broadcast_to(p, (128, 128)).T * freq[0:1, :]
    span = pl.ds(first, 128)
    cos[span, :] = jnp.cos(angles)
    s = jnp.sin(angles)
    sin[span, :] = jnp.where((lane_of(128) & 32) == 0, -s, s)


def project_rows(first, rows, lat, key_up, value_up, kslot, krot, values):
    span = pl.ds(first, rows)
    low = lane_of(rows) < 64
    compressed = lat[span, :D_C]
    both = lat[span, D_C:].astype(F32)
    krot[span, :] = jnp.where(low, both, 0.0).astype(BF16)

    def pair(p, _):
        source = pl.ds(pl.multiple_of(p * 256, 256), 256)
        keys = dot(compressed, key_up[:, source], NN)
        values[span, source] = dot(compressed, value_up[:, source], NN).astype(BF16)
        turned = pltpu.roll(keys[:, 128:], 64, 1)
        kslot[span, pl.ds(pl.multiple_of(p * 384, 128), 128)] = keys[:, :128].astype(BF16)
        kslot[span, pl.ds(pl.multiple_of(p * 384 + 128, 128), 128)] = jnp.where(low, 0.0, turned).astype(BF16)
        kslot[span, pl.ds(pl.multiple_of(p * 384 + 256, 128), 128)] = jnp.where(low, turned, both).astype(BF16)
        return 0

    lax.fori_loop(0, key_up.shape[1] // 256, pair, 0)


def turn_queries(first, rows, pairs, qbuf, cos, sin):
    span = pl.ds(first, rows)
    low = lane_of(rows) < 64
    c, s = cos[span, :], sin[span, :]

    def pair(p, _):
        at1 = pl.ds(pl.multiple_of(p * 384 + 128, 128), 128)
        at2 = pl.ds(pl.multiple_of(p * 384 + 256, 128), 128)
        one, two = qbuf[span, at1].astype(F32), qbuf[span, at2].astype(F32)
        m = jnp.where(low, one, two)
        r = m * c + swap_halves(m) * s
        qbuf[span, at1] = jnp.where(low, r, one).astype(BF16)
        qbuf[span, at2] = jnp.where(low, two, r).astype(BF16)
        return 0

    lax.fori_loop(*pairs, pair, 0)


def fill_bias(first, pos, bias):
    for half in range(2):
        p = pos[0:1, pl.ds(pl.multiple_of(first + half * 128, 128), 128)]
        c = lax.broadcasted_iota(jnp.int32, (384, 128), 0)
        r = lax.broadcasted_iota(jnp.int32, (384, 128), 1) + 256
        seen = (c <= r) & (c >= r - p)
        bias[half] = jnp.where(seen, 0.0, BIG)


def weigh(scores, dprob, bias):
    probs, grads = [], []
    for half in range(2):
        rows, cols = slice(128 * half, 128 * half + 384), slice(128 * half, 128 * half + 128)
        s = scores[rows, cols] + bias[half]
        d = dprob[rows, cols]
        top = jnp.max(s, axis=0, keepdims=True)
        e = jnp.exp((s - top) * SCALING)
        total = jnp.sum(e, axis=0, keepdims=True)
        delta = jnp.sum(e * d, axis=0, keepdims=True) / total
        prob = e * (1.0 / total)
        grad = (prob * (d - delta) * SCALING).astype(BF16)
        prob = prob.astype(BF16)
        none = jnp.zeros((128, 128), BF16)
        order = (lambda x: [x, none]) if half == 0 else (lambda x: [none, x])
        probs.append(jnp.concatenate(order(prob), axis=0))
        grads.append(jnp.concatenate(order(grad), axis=0))
    return jnp.concatenate(probs, axis=1), jnp.concatenate(grads, axis=1)


def attend(first, pairs, qbuf, gout, kslot, krot, values, bias, cos, sin, dq, dkacc, dvacc):
    qs, ks = pl.ds(first, 256), pl.ds(first, 512)

    def pair(p, _):
        s0 = pl.multiple_of(p * 384, 128)
        v0 = pl.multiple_of(p * 256, 256)
        q = qbuf[qs, pl.ds(s0, 384)]
        g = gout[qs, pl.ds(v0, 256)]
        k0 = jnp.concatenate([kslot[ks, pl.ds(s0, 128)], krot[ks, :]], axis=1)
        k1 = kslot[ks, pl.ds(pl.multiple_of(s0 + 128, 128), 256)]
        dqs, dks = [], []
        for odd, k in ((0, k0), (1, k1)):
            qh = q[:, 128 * odd : 128 * odd + 256]
            gh = g[:, 128 * odd : 128 * odd + 128]
            vh = values[ks, pl.ds(pl.multiple_of(v0 + 128 * odd, 128), 128)]
            scores = dot(k, qh, NT)
            dprob = dot(vh, gh, NT)
            prob, grad = weigh(scores, dprob, bias)
            dvacc[ks, pl.ds(pl.multiple_of(v0 + 128 * odd, 128), 128)] += dot(prob, gh, NN)
            dks.append(dot(grad, qh, NN))
            dqs.append(dot(grad, k, TN))
        low = lane_of(512) < 64
        dkacc[ks, pl.ds(s0, 128)] += dks[0][:, :128]
        dkacc[ks, pl.ds(pl.multiple_of(s0 + 128, 128), 128)] += jnp.where(low, dks[0][:, 128:], dks[1][:, :128])
        dkacc[ks, pl.ds(pl.multiple_of(s0 + 256, 128), 128)] += dks[1][:, 128:]
        low = lane_of(256) < 64
        one, two = dqs[0][:, 128:] + dqs[1][:, :128], dqs[1][:, 128:]
        m = jnp.where(low, one, two)
        r = m * cos[qs, :] - swap_halves(m) * sin[qs, :]
        dq[qs, pl.ds(s0, 128)] = dqs[0][:, :128].astype(BF16)
        dq[qs, pl.ds(pl.multiple_of(s0 + 128, 128), 128)] = jnp.where(low, r, one).astype(BF16)
        dq[qs, pl.ds(pl.multiple_of(s0 + 256, 128), 128)] = jnp.where(low, two, r).astype(BF16)
        return 0

    lax.fori_loop(*pairs, pair, 0)


def gather_back(first, rows, key_up, value_up, dkacc, dvacc):
    span = pl.ds(first, rows)
    low = lane_of(rows) < 64
    total = jnp.zeros((rows, D_C), F32)
    turn = jnp.zeros((rows, LANES), F32)
    for p in range(key_up.shape[1] // 256):
        one = dkacc[span, 384 * p + 128 : 384 * p + 256]
        two = dkacc[span, 384 * p + 256 : 384 * p + 384]
        turn = turn + jnp.where(low, one, two)
        odd = pltpu.roll(jnp.where(low, two, one), 64, 1).astype(BF16)
        even = dkacc[span, 384 * p : 384 * p + 128].astype(BF16)
        cols = slice(256 * p, 256 * p + 256)
        total = total + dot(jnp.concatenate([even, odd], axis=1), key_up[:, cols], NT)
        total = total + dot(dvacc[span, cols].astype(BF16), value_up[:, cols], NT)
    return total, turn + pltpu.roll(turn, 64, 1)


STEPS = ((0, 1), (1, 0), (1, 1), (3, 0), (3, 1), (2, 0), (2, 1))


def kernel(
    query, gout_hbm, lat_in, pos, key_hbm, value_hbm, freq, dq_hbm, glat,
    qbuf, lat, gout, key_up, value_up, cos, sin, kslot, krot, values, bias, dkacc, dvacc, dq, sbuf, own, rbuf, hbuf,
    load_sem, store_sem, lat_send, lat_recv, q_send, q_recv, g_send, g_recv, h_send, h_recv,
):
    g, b = lax.axis_index("grp"), lax.axis_index("blk")
    nb = lax.axis_size("blk")
    z, y = g // 2, g % 2
    slots = qbuf.shape[1]
    group_tok = qbuf.shape[0]
    ahead, behind = (b + 1) % nb, (b + nb - 1) % nb

    def peer(step):
        return ((z + step[0]) % 4) * 2 + (y + step[1]) % 2

    def remote(src, dst, send, recv, to_g=None, to_b=None):
        return pltpu.make_async_remote_copy(
            src_ref=src,
            dst_ref=dst,
            send_sem=send,
            recv_sem=recv,
            device_id=(g if to_g is None else to_g, b if to_b is None else to_b),
            device_id_type=pl.DeviceIdType.MESH,
        )

    loads = [
        pltpu.make_async_copy(key_hbm, key_up, load_sem.at[0]),
        pltpu.make_async_copy(value_hbm, value_up, load_sem.at[1]),
        pltpu.make_async_copy(
            query.at[:, pl.ds(pl.multiple_of(g * slots, 128), slots)],
            qbuf.at[pl.ds(pl.multiple_of(g * 128, 128), 128), :],
            load_sem.at[2],
        ),
        pltpu.make_async_copy(gout_hbm, gout, load_sem.at[3]),
    ]

    barrier = pltpu.get_barrier_semaphore()
    for step in STEPS:
        pl.semaphore_signal(barrier, inc=1, device_id=(peer(step), b), device_id_type=pl.DeviceIdType.MESH)
    for other in (ahead, behind):
        pl.semaphore_signal(barrier, inc=1, device_id=(g, other), device_id_type=pl.DeviceIdType.MESH)

    my = pl.multiple_of(g * 128, 128)
    mine = pl.ds(my, 128)
    fill_tables(my, pos, freq, cos, sin)

    def rows_of(gg):
        return pl.ds(pl.multiple_of(256 + gg * 128, 128), 128)

    raw = lat_in[D_C:, :].astype(F32)
    raw = jnp.concatenate([raw, raw], axis=0).T
    turned = (raw * cos[mine, :] + swap_halves(raw) * sin[mine, :]).astype(BF16)
    lat[rows_of(g), :D_C] = lat_in[:D_C, :].astype(F32).T.astype(BF16)
    lat[rows_of(g), D_C:] = turned

    pl.semaphore_wait(barrier, 9)

    def lat_copy(i, of_g, to_g):
        return remote(lat.at[rows_of(of_g), :], lat.at[rows_of(of_g), :], lat_send.at[i], lat_recv.at[i], to_g=to_g)

    mate = z * 2 + 1 - y
    first_copies = [lat_copy(0, g, mate)] + [
        lat_copy(1 + i, g, peer((dz, 0))) for i, dz in enumerate((1, 3, 2))
    ]
    for copy in first_copies:
        copy.start()
    half = slots // 2
    q_copies = {}
    for dz, dy in STEPS:
        for part in (0, 1) if dz == 2 else (None,):
            n = len(q_copies)
            begin, count = (0, slots) if part is None else (part * half, half)
            q_copies[(dz, dy, part)] = remote(
                query.at[:, pl.ds(pl.multiple_of(peer((dz, dy)) * slots + begin, 128), count)],
                qbuf.at[mine, begin : begin + count],
                q_send.at[n],
                q_recv.at[n],
                to_g=peer((dz, dy)),
            )
    q_copies[(0, 1, None)].start()
    for load in loads:
        load.start()
    first_copies[0].wait_recv()
    second_copies = [lat_copy(4 + i, mate, peer((dz, 0))) for i, dz in enumerate((1, 3, 2))]
    for copy in second_copies:
        copy.start()
    lat_copies = first_copies + second_copies

    dkacc[...] = jnp.zeros_like(dkacc)
    dvacc[...] = jnp.zeros_like(dvacc)

    def table(t, _):
        fill_tables(pl.multiple_of(t * 128, 128), pos, freq, cos, sin)
        return 0

    lax.fori_loop(0, group_tok // 128, table, 0)

    for copy in lat_copies:
        copy.wait_send()
    for copy in lat_copies[1:]:
        copy.wait_recv()
    halo = remote(lat.at[pl.ds(group_tok, 256), :], lat.at[pl.ds(0, 256), :], h_send.at[0], h_recv.at[0], to_b=ahead)
    halo.start()
    for step in ((1, 0), (3, 0), (1, 1), (3, 1)):
        q_copies[(*step, None)].start()
    loads[0].wait()
    loads[1].wait()

    project_rows(256, group_tok, lat, key_up, value_up, kslot, krot, values)
    loads[2].wait()
    loads[3].wait()
    halo.wait_recv()
    project_rows(0, 256, lat, key_up, value_up, kslot, krot, values)

    back = remote(sbuf.at[0:256, :], hbuf, h_send.at[1], h_recv.at[1], to_b=behind)
    g_copies = []

    def return_halo():
        total, turn = gather_back(0, 256, key_up, value_up, dkacc, dvacc)
        sbuf[0:256, :D_C] = total.astype(BF16)
        sbuf[0:256, D_C:] = turn.astype(BF16)
        back.start()

    def send_back(way):
        block = (z + way) % 4
        first = pl.multiple_of(256 + block * 256, 256)
        total, turn = gather_back(first, 256, key_up, value_up, dkacc, dvacc)
        if way:
            sbuf[pl.ds(first, 256), :D_C] = total.astype(BF16)
            sbuf[pl.ds(first, 256), D_C:] = turn.astype(BF16)
        else:
            own[:, :D_C] = total
            own[:, D_C:] = turn

        @pl.when(block == 3)
        def _():
            back.wait_recv()
            if way:
                sbuf[pl.ds(first, 256), :] = (sbuf[pl.ds(first, 256), :].astype(F32) + hbuf[...].astype(F32)).astype(BF16)
            else:
                own[...] += hbuf[...].astype(F32)

        if not way:
            row = pl.multiple_of((1 - y) * 128, 128)
            sbuf[pl.ds(pl.multiple_of(first + row, 128), 128), :] = own[pl.ds(row, 128), :].astype(BF16)
        for i, step in enumerate(STEPS):
            if step[0] == way:
                copy = remote(sbuf.at[rows_of(peer(step)), :], rbuf.at[i], g_send.at[i], g_recv.at[i], to_g=peer(step))
                copy.start()
                g_copies.append(copy)

    stores = []
    for i, way in enumerate((0, 3, 1, 2)):
        block = (z + way) % 4
        first = pl.multiple_of(block * 256, 256)
        for part in (0, 1) if way == 2 else (None,):
            for dy in (0, 1):
                if way or dy:
                    q_copies[((4 - way) % 4, dy, part)].wait_recv()
            pairs = (0, slots // 384) if part is None else (part * slots // 768, (part + 1) * slots // 768)
            turn_queries(first, 256, pairs, qbuf, cos, sin)
            if not part:
                fill_bias(first, pos, bias)
            attend(first, pairs, qbuf, gout, kslot, krot, values, bias, cos, sin, dq, dkacc, dvacc)
        store = pltpu.make_async_copy(dq.at[pl.ds(first, 256), :], dq_hbm.at[pl.ds(first, 256), :], store_sem.at[i])
        store.start()
        stores.append(store)
        if i == 0:
            for part in (0, 1):
                q_copies[(2, 0, part)].start()
                q_copies[(2, 1, part)].start()
        pl.when(block == 0)(return_halo)
        if i == 1:
            send_back(3)
        if i == 2:
            send_back(0)
        if i == 3:
            send_back(2)
            send_back(1)

    total = own[pl.ds(pl.multiple_of(y * 128, 128), 128), :]
    for copy in g_copies:
        copy.wait_recv()
    for i in range(len(STEPS)):
        total = total + rbuf[i].astype(F32)
    turn = total[:, D_C:]
    turn = turn * cos[mine, :] - swap_halves(turn) * sin[mine, :]
    glat[:D_C, :] = total[:, :D_C].T.astype(BF16)
    glat[D_C:, :] = turn.T[:D_R, :].astype(BF16)

    for copy in list(q_copies.values()) + g_copies + [halo, back]:
        copy.wait_send()
    for store in stores:
        store.wait()


def per_device(query, latent, positions, key_up, value_up, grad_out):
    tok_dev = query.shape[1]
    group_tok = tok_dev * lax.axis_size("grp")
    key_rows = 256 + group_tok
    slots = query.shape[2] // lax.axis_size("grp")
    width = key_up.shape[1]
    wide = D_C + LANES
    freq = jnp.asarray(np.tile(freqs_of(D_R), 4)[None])
    hbm, vmem = pl.BlockSpec(memory_space=pl.ANY), pl.BlockSpec(memory_space=pltpu.VMEM)
    dma = pltpu.SemaphoreType.DMA
    grad_query, grad_latent = pl.pallas_call(
        kernel,
        out_shape=(
            jax.ShapeDtypeStruct((group_tok, slots), BF16),
            jax.ShapeDtypeStruct((D_C + D_R, tok_dev), BF16),
        ),
        in_specs=[hbm, hbm, vmem, vmem, hbm, hbm, vmem],
        out_specs=(hbm, vmem),
        scratch_shapes=[
            pltpu.VMEM((group_tok, slots), BF16),
            pltpu.VMEM((key_rows, wide), BF16),
            pltpu.VMEM((group_tok, width), BF16),
            pltpu.VMEM((D_C, width), BF16),
            pltpu.VMEM((D_C, width), BF16),
            pltpu.VMEM((group_tok, LANES), F32),
            pltpu.VMEM((group_tok, LANES), F32),
            pltpu.VMEM((key_rows, slots), BF16),
            pltpu.VMEM((key_rows, LANES), BF16),
            pltpu.VMEM((key_rows, width), BF16),
            pltpu.VMEM((2, 384, 128), F32),
            pltpu.VMEM((key_rows, slots), F32),
            pltpu.VMEM((key_rows, width), F32),
            pltpu.VMEM((group_tok, slots), BF16),
            pltpu.VMEM((key_rows, wide), BF16),
            pltpu.VMEM((256, wide), F32),
            pltpu.VMEM((7, tok_dev, wide), BF16),
            pltpu.VMEM((256, wide), BF16),
            dma((4,)),
            dma((4,)),
            dma((7,)),
            dma((7,)),
            dma((9,)),
            dma((9,)),
            dma((7,)),
            dma((7,)),
            dma((2,)),
            dma((2,)),
        ],
        compiler_params=pltpu.CompilerParams(
            vmem_limit_bytes=60 * 1024 * 1024, collective_id=0, has_side_effects=True
        ),
    )(query[0], grad_out[0], latent[0].T, positions, key_up, value_up, freq)
    return (grad_query[None], grad_latent.T[None])


def solution(mesh):
    placed = (
        P("blk", "grp", None),
        P("blk", "grp", None),
        P("blk", None),
        P(None, "grp"),
        P(None, "grp"),
        P("blk", None, "grp"),
    )
    return jax.shard_map(
        per_device,
        mesh=mesh,
        in_specs=placed,
        out_specs=(P("blk", None, "grp"), P("blk", "grp", None)),
        check_vma=False,
    )
```

```python
import math

import jax
import jax.numpy as jnp
import numpy as np
from jax import lax
from jax.experimental import pallas as pl
from jax.experimental.pallas import tpu as pltpu
from jax.sharding import PartitionSpec as P

D_C = 512
D_R = 64
D_N = 128
D_V = 128
LANES = 128
BIG = -1e30

rope_base = 10000.0
yarn_factor = 40.0
pretrain_context = 4096.0

mscale = 0.1 * math.log(yarn_factor) + 1.0
SCALING = (D_N + D_R) ** (-0.5) * mscale * mscale

F32 = jnp.float32
BF16 = jnp.bfloat16
NT = (((1,), (1,)), ((), ()))
TN = (((0,), (0,)), ((), ()))
NN = (((1,), (0,)), ((), ()))


def dot(a, b, dims):
    return lax.dot_general(a, b, dims, preferred_element_type=F32)


def freqs_of(width):
    half_width = width // 2
    index = np.arange(half_width, dtype=np.float64)
    extrapolated = rope_base ** (-2.0 * index / width)
    span = 2.0 * math.log(rope_base)
    lowest = max(math.floor(width * math.log(pretrain_context / (64.0 * math.pi)) / span), 0)
    highest = min(math.ceil(width * math.log(pretrain_context / (2.0 * math.pi)) / span), width - 1)
    ramp = np.clip((index - lowest) / (highest - lowest), 0.0, 1.0)
    return (extrapolated / yarn_factor * ramp + extrapolated * (1.0 - ramp)).astype(np.float32)


def lane_of(rows):
    return lax.broadcasted_iota(jnp.int32, (rows, LANES), 1)


def swap_halves(m):
    lane = lane_of(m.shape[0])
    return jnp.where((lane & 32) == 0, pltpu.roll(m, 96, 1), pltpu.roll(m, 32, 1))


def fill_tables(first, pos, freq, cos, sin):
    p = pos[0:1, pl.ds(pl.multiple_of(first, 128), 128)].astype(F32)
    angles = jnp.broadcast_to(p, (128, 128)).T * freq[0:1, :]
    span = pl.ds(first, 128)
    cos[span, :] = jnp.cos(angles)
    s = jnp.sin(angles)
    sin[span, :] = jnp.where((lane_of(128) & 32) == 0, -s, s)


def project_rows(first, rows, lat, key_up, value_up, kslot, krot, values):
    span = pl.ds(first, rows)
    low = lane_of(rows) < 64
    compressed = lat[span, :D_C]
    both = lat[span, D_C:].astype(F32)
    krot[span, :] = jnp.where(low, both, 0.0).astype(BF16)

    def pair(p, _):
        source = pl.ds(pl.multiple_of(p * 256, 256), 256)
        keys = dot(compressed, key_up[:, source], NN)
        values[span, source] = dot(compressed, value_up[:, source], NN).astype(BF16)
        turned = pltpu.roll(keys[:, 128:], 64, 1)
        kslot[span, pl.ds(pl.multiple_of(p * 384, 128), 128)] = keys[:, :128].astype(BF16)
        kslot[span, pl.ds(pl.multiple_of(p * 384 + 128, 128), 128)] = jnp.where(low, 0.0, turned).astype(BF16)
        kslot[span, pl.ds(pl.multiple_of(p * 384 + 256, 128), 128)] = jnp.where(low, turned, both).astype(BF16)
        return 0

    lax.fori_loop(0, key_up.shape[1] // 256, pair, 0)


def turn_queries(first, rows, pairs, qbuf, cos, sin):
    span = pl.ds(first, rows)
    low = lane_of(rows) < 64
    c, s = cos[span, :], sin[span, :]

    def pair(p, _):
        at1 = pl.ds(pl.multiple_of(p * 384 + 128, 128), 128)
        at2 = pl.ds(pl.multiple_of(p * 384 + 256, 128), 128)
        one, two = qbuf[span, at1].astype(F32), qbuf[span, at2].astype(F32)
        m = jnp.where(low, one, two)
        r = m * c + swap_halves(m) * s
        qbuf[span, at1] = jnp.where(low, r, one).astype(BF16)
        qbuf[span, at2] = jnp.where(low, two, r).astype(BF16)
        return 0

    lax.fori_loop(*pairs, pair, 0)


def fill_bias(first, pos, bias):
    for half in range(2):
        p = pos[0:1, pl.ds(pl.multiple_of(first + half * 128, 128), 128)]
        c = lax.broadcasted_iota(jnp.int32, (384, 128), 0)
        r = lax.broadcasted_iota(jnp.int32, (384, 128), 1) + 256
        seen = (c <= r) & (c >= r - p)
        bias[half] = jnp.where(seen, 0.0, BIG)


def weigh(scores, dprob, bias):
    probs, grads = [], []
    for half in range(2):
        rows, cols = slice(128 * half, 128 * half + 384), slice(128 * half, 128 * half + 128)
        s = scores[rows, cols] + bias[half]
        d = dprob[rows, cols]
        top = jnp.max(s, axis=0, keepdims=True)
        e = jnp.exp2((s - top) * (SCALING * math.log2(math.e)))
        total = jnp.sum(e, axis=0, keepdims=True)
        share = 1.0 / total
        delta = jnp.sum(e * d, axis=0, keepdims=True) * share
        prob = e * share
        grad = (prob * ((d - delta) * SCALING)).astype(BF16)
        prob = prob.astype(BF16)
        none = jnp.zeros((128, 128), BF16)
        order = (lambda x: [x, none]) if half == 0 else (lambda x: [none, x])
        probs.append(jnp.concatenate(order(prob), axis=0))
        grads.append(jnp.concatenate(order(grad), axis=0))
    return jnp.concatenate(probs, axis=1), jnp.concatenate(grads, axis=1)


def attend(first, pairs, qbuf, gout, kslot, krot, values, bias, cos, sin, dq, dkacc, dvacc):
    qs, ks = pl.ds(first, 256), pl.ds(first, 512)

    def pair(p, _):
        s0 = pl.multiple_of(p * 384, 128)
        v0 = pl.multiple_of(p * 256, 256)
        q = qbuf[qs, pl.ds(s0, 384)]
        g = gout[qs, pl.ds(v0, 256)]
        k0 = jnp.concatenate([kslot[ks, pl.ds(s0, 128)], krot[ks, :]], axis=1)
        k1 = kslot[ks, pl.ds(pl.multiple_of(s0 + 128, 128), 256)]
        dqs, dks = [], []
        for odd, k in ((0, k0), (1, k1)):
            qh = q[:, 128 * odd : 128 * odd + 256]
            gh = g[:, 128 * odd : 128 * odd + 128]
            vh = values[ks, pl.ds(pl.multiple_of(v0 + 128 * odd, 128), 128)]
            scores = dot(k, qh, NT)
            dprob = dot(vh, gh, NT)
            prob, grad = weigh(scores, dprob, bias)
            dvacc[ks, pl.ds(pl.multiple_of(v0 + 128 * odd, 128), 128)] += dot(prob, gh, NN)
            dks.append(dot(grad, qh, NN))
            dqs.append(dot(grad, k, TN))
        low = lane_of(512) < 64
        dkacc[ks, pl.ds(s0, 128)] += dks[0][:, :128]
        dkacc[ks, pl.ds(pl.multiple_of(s0 + 128, 128), 128)] += jnp.where(low, dks[0][:, 128:], dks[1][:, :128])
        dkacc[ks, pl.ds(pl.multiple_of(s0 + 256, 128), 128)] += dks[1][:, 128:]
        low = lane_of(256) < 64
        one, two = dqs[0][:, 128:] + dqs[1][:, :128], dqs[1][:, 128:]
        m = jnp.where(low, one, two)
        r = m * cos[qs, :] - swap_halves(m) * sin[qs, :]
        dq[qs, pl.ds(s0, 128)] = dqs[0][:, :128].astype(BF16)
        dq[qs, pl.ds(pl.multiple_of(s0 + 128, 128), 128)] = jnp.where(low, r, one).astype(BF16)
        dq[qs, pl.ds(pl.multiple_of(s0 + 256, 128), 128)] = jnp.where(low, two, r).astype(BF16)
        return 0

    lax.fori_loop(*pairs, pair, 0, unroll=2)


def gather_back(first, rows, key_up, value_up, dkacc, dvacc):
    span = pl.ds(first, rows)
    low = lane_of(rows) < 64
    total = jnp.zeros((rows, D_C), F32)
    turn = jnp.zeros((rows, LANES), F32)
    for p in range(key_up.shape[1] // 256):
        one = dkacc[span, 384 * p + 128 : 384 * p + 256]
        two = dkacc[span, 384 * p + 256 : 384 * p + 384]
        turn = turn + jnp.where(low, one, two)
        odd = pltpu.roll(jnp.where(low, two, one), 64, 1).astype(BF16)
        even = dkacc[span, 384 * p : 384 * p + 128].astype(BF16)
        cols = slice(256 * p, 256 * p + 256)
        total = total + dot(jnp.concatenate([even, odd], axis=1), key_up[:, cols], NT)
        total = total + dot(dvacc[span, cols].astype(BF16), value_up[:, cols], NT)
    return total, turn + pltpu.roll(turn, 64, 1)


STEPS = ((0, 1), (1, 0), (1, 1), (3, 0), (3, 1), (2, 0), (2, 1))


def kernel(
    query, gout_hbm, lat_in, pos, key_hbm, value_hbm, freq, dq_hbm, glat,
    qbuf, lat, gout, key_up, value_up, cos, sin, kslot, krot, values, bias, dkacc, dvacc, dq, sbuf, own, rbuf, hbuf,
    load_sem, store_sem, lat_send, lat_recv, q_send, q_recv, g_send, g_recv, h_send, h_recv,
):
    g, b = lax.axis_index("grp"), lax.axis_index("blk")
    nb = lax.axis_size("blk")
    z, y = g // 2, g % 2
    slots = qbuf.shape[1]
    group_tok = qbuf.shape[0]
    ahead, behind = (b + 1) % nb, (b + nb - 1) % nb

    def peer(step):
        return ((z + step[0]) % 4) * 2 + (y + step[1]) % 2

    def remote(src, dst, send, recv, to_g=None, to_b=None):
        return pltpu.make_async_remote_copy(
            src_ref=src,
            dst_ref=dst,
            send_sem=send,
            recv_sem=recv,
            device_id=(g if to_g is None else to_g, b if to_b is None else to_b),
            device_id_type=pl.DeviceIdType.MESH,
        )

    loads = [
        pltpu.make_async_copy(key_hbm, key_up, load_sem.at[0]),
        pltpu.make_async_copy(value_hbm, value_up, load_sem.at[1]),
        pltpu.make_async_copy(
            query.at[:, pl.ds(pl.multiple_of(g * slots, 128), slots)],
            qbuf.at[pl.ds(pl.multiple_of(g * 128, 128), 128), :],
            load_sem.at[2],
        ),
        pltpu.make_async_copy(gout_hbm, gout, load_sem.at[3]),
    ]

    barrier = pltpu.get_barrier_semaphore()
    for step in STEPS:
        pl.semaphore_signal(barrier, inc=1, device_id=(peer(step), b), device_id_type=pl.DeviceIdType.MESH)
    for other in (ahead, behind):
        pl.semaphore_signal(barrier, inc=1, device_id=(g, other), device_id_type=pl.DeviceIdType.MESH)

    my = pl.multiple_of(g * 128, 128)
    mine = pl.ds(my, 128)
    fill_tables(my, pos, freq, cos, sin)

    def rows_of(gg):
        return pl.ds(pl.multiple_of(256 + gg * 128, 128), 128)

    raw = lat_in[D_C:, :].astype(F32)
    raw = jnp.concatenate([raw, raw], axis=0).T
    turned = (raw * cos[mine, :] + swap_halves(raw) * sin[mine, :]).astype(BF16)
    lat[rows_of(g), :D_C] = lat_in[:D_C, :].astype(F32).T.astype(BF16)
    lat[rows_of(g), D_C:] = turned

    pl.semaphore_wait(barrier, 9)

    def lat_copy(i, of_g, to_g):
        return remote(lat.at[rows_of(of_g), :], lat.at[rows_of(of_g), :], lat_send.at[i], lat_recv.at[i], to_g=to_g)

    mate = z * 2 + 1 - y
    first_copies = [lat_copy(0, g, mate)] + [
        lat_copy(1 + i, g, peer((dz, 0))) for i, dz in enumerate((1, 3, 2))
    ]
    for copy in first_copies:
        copy.start()
    half = slots // 2
    q_copies = {}
    for dz, dy in STEPS:
        for part in (0, 1) if dz == 2 else (None,):
            n = len(q_copies)
            begin, count = (0, slots) if part is None else (part * half, half)
            q_copies[(dz, dy, part)] = remote(
                query.at[:, pl.ds(pl.multiple_of(peer((dz, dy)) * slots + begin, 128), count)],
                qbuf.at[mine, begin : begin + count],
                q_send.at[n],
                q_recv.at[n],
                to_g=peer((dz, dy)),
            )
    q_copies[(0, 1, None)].start()
    for load in loads:
        load.start()
    first_copies[0].wait_recv()
    second_copies = [lat_copy(4 + i, mate, peer((dz, 0))) for i, dz in enumerate((1, 3, 2))]
    for copy in second_copies:
        copy.start()
    lat_copies = first_copies + second_copies

    dkacc[...] = jnp.zeros_like(dkacc)
    dvacc[...] = jnp.zeros_like(dvacc)

    def table(t, _):
        fill_tables(pl.multiple_of(t * 128, 128), pos, freq, cos, sin)
        return 0

    lax.fori_loop(0, group_tok // 128, table, 0)

    for copy in lat_copies:
        copy.wait_send()
    for copy in lat_copies[1:]:
        copy.wait_recv()
    halo = remote(lat.at[pl.ds(group_tok, 256), :], lat.at[pl.ds(0, 256), :], h_send.at[0], h_recv.at[0], to_b=ahead)
    halo.start()
    for step in ((1, 0), (3, 0), (1, 1), (3, 1)):
        q_copies[(*step, None)].start()
    loads[0].wait()
    loads[1].wait()

    project_rows(256, group_tok, lat, key_up, value_up, kslot, krot, values)
    loads[2].wait()
    loads[3].wait()
    halo.wait_recv()
    project_rows(0, 256, lat, key_up, value_up, kslot, krot, values)

    back = remote(sbuf.at[0:256, :], hbuf, h_send.at[1], h_recv.at[1], to_b=behind)
    g_copies = []

    def return_halo():
        total, turn = gather_back(0, 256, key_up, value_up, dkacc, dvacc)
        sbuf[0:256, :D_C] = total.astype(BF16)
        sbuf[0:256, D_C:] = turn.astype(BF16)
        back.start()

    def send_back(way):
        block = (z + way) % 4
        first = pl.multiple_of(256 + block * 256, 256)
        total, turn = gather_back(first, 256, key_up, value_up, dkacc, dvacc)
        if way:
            sbuf[pl.ds(first, 256), :D_C] = total.astype(BF16)
            sbuf[pl.ds(first, 256), D_C:] = turn.astype(BF16)
        else:
            own[:, :D_C] = total
            own[:, D_C:] = turn

        @pl.when(block == 3)
        def _():
            back.wait_recv()
            if way:
                sbuf[pl.ds(first, 256), :] = (sbuf[pl.ds(first, 256), :].astype(F32) + hbuf[...].astype(F32)).astype(BF16)
            else:
                own[...] += hbuf[...].astype(F32)

        if not way:
            row = pl.multiple_of((1 - y) * 128, 128)
            sbuf[pl.ds(pl.multiple_of(first + row, 128), 128), :] = own[pl.ds(row, 128), :].astype(BF16)
        for i, step in enumerate(STEPS):
            if step[0] == way:
                copy = remote(sbuf.at[rows_of(peer(step)), :], rbuf.at[i], g_send.at[i], g_recv.at[i], to_g=peer(step))
                copy.start()
                g_copies.append(copy)

    stores = []
    for i, way in enumerate((0, 3, 1, 2)):
        block = (z + way) % 4
        first = pl.multiple_of(block * 256, 256)
        for part in (0, 1) if way == 2 else (None,):
            for dy in (0, 1):
                if way or dy:
                    q_copies[((4 - way) % 4, dy, part)].wait_recv()
            pairs = (0, slots // 384) if part is None else (part * slots // 768, (part + 1) * slots // 768)
            turn_queries(first, 256, pairs, qbuf, cos, sin)
            if not part:
                fill_bias(first, pos, bias)
            attend(first, pairs, qbuf, gout, kslot, krot, values, bias, cos, sin, dq, dkacc, dvacc)
        store = pltpu.make_async_copy(dq.at[pl.ds(first, 256), :], dq_hbm.at[pl.ds(first, 256), :], store_sem.at[i])
        store.start()
        stores.append(store)
        if i == 0:
            for part in (0, 1):
                q_copies[(2, 0, part)].start()
                q_copies[(2, 1, part)].start()
        if i < 3:
            pl.when(block == 0)(return_halo)
        if i == 1:
            send_back(3)
        if i == 2:
            send_back(0)
        if i == 3:
            send_back(2)
            pl.when(block == 0)(return_halo)
            send_back(1)

    total = own[pl.ds(pl.multiple_of(y * 128, 128), 128), :]
    for copy in g_copies:
        copy.wait_recv()
    for i in range(len(STEPS)):
        total = total + rbuf[i].astype(F32)
    turn = total[:, D_C:]
    turn = turn * cos[mine, :] - swap_halves(turn) * sin[mine, :]
    glat[:D_C, :] = total[:, :D_C].T.astype(BF16)
    glat[D_C:, :] = turn.T[:D_R, :].astype(BF16)

    for copy in list(q_copies.values()) + g_copies + [halo, back]:
        copy.wait_send()
    for store in stores:
        store.wait()


def per_device(query, latent, positions, key_up, value_up, grad_out):
    tok_dev = query.shape[1]
    group_tok = tok_dev * lax.axis_size("grp")
    key_rows = 256 + group_tok
    slots = query.shape[2] // lax.axis_size("grp")
    width = key_up.shape[1]
    wide = D_C + LANES
    freq = jnp.asarray(np.tile(freqs_of(D_R), 4)[None])
    hbm, vmem = pl.BlockSpec(memory_space=pl.ANY), pl.BlockSpec(memory_space=pltpu.VMEM)
    dma = pltpu.SemaphoreType.DMA
    grad_query, grad_latent = pl.pallas_call(
        kernel,
        out_shape=(
            jax.ShapeDtypeStruct((group_tok, slots), BF16),
            jax.ShapeDtypeStruct((D_C + D_R, tok_dev), BF16),
        ),
        in_specs=[hbm, hbm, vmem, vmem, hbm, hbm, vmem],
        out_specs=(hbm, vmem),
        scratch_shapes=[
            pltpu.VMEM((group_tok, slots), BF16),
            pltpu.VMEM((key_rows, wide), BF16),
            pltpu.VMEM((group_tok, width), BF16),
            pltpu.VMEM((D_C, width), BF16),
            pltpu.VMEM((D_C, width), BF16),
            pltpu.VMEM((group_tok, LANES), F32),
            pltpu.VMEM((group_tok, LANES), F32),
            pltpu.VMEM((key_rows, slots), BF16),
            pltpu.VMEM((key_rows, LANES), BF16),
            pltpu.VMEM((key_rows, width), BF16),
            pltpu.VMEM((2, 384, 128), F32),
            pltpu.VMEM((key_rows, slots), F32),
            pltpu.VMEM((key_rows, width), F32),
            pltpu.VMEM((group_tok, slots), BF16),
            pltpu.VMEM((key_rows, wide), BF16),
            pltpu.VMEM((256, wide), F32),
            pltpu.VMEM((7, tok_dev, wide), BF16),
            pltpu.VMEM((256, wide), BF16),
            dma((4,)),
            dma((4,)),
            dma((7,)),
            dma((7,)),
            dma((9,)),
            dma((9,)),
            dma((7,)),
            dma((7,)),
            dma((2,)),
            dma((2,)),
        ],
        compiler_params=pltpu.CompilerParams(
            vmem_limit_bytes=60 * 1024 * 1024, collective_id=0, has_side_effects=True
        ),
    )(query[0], grad_out[0], latent[0].T, positions, key_up, value_up, freq)
    return (grad_query[None], grad_latent.T[None])


def solution(mesh):
    placed = (
        P("blk", "grp", None),
        P("blk", "grp", None),
        P("blk", None),
        P(None, "grp"),
        P(None, "grp"),
        P("blk", None, "grp"),
    )
    return jax.shard_map(
        per_device,
        mesh=mesh,
        in_specs=placed,
        out_specs=(P("blk", None, "grp"), P("blk", "grp", None)),
        check_vma=False,
    )
```

```python
import math

import jax
import jax.numpy as jnp
import numpy as np
from jax import lax
from jax.experimental import pallas as pl
from jax.experimental.pallas import tpu as pltpu
from jax.sharding import PartitionSpec as P

D_C = 512
D_R = 64
D_N = 128
D_V = 128
LANES = 128
BIG = -1e30

rope_base = 10000.0
yarn_factor = 40.0
pretrain_context = 4096.0

mscale = 0.1 * math.log(yarn_factor) + 1.0
SCALING = (D_N + D_R) ** (-0.5) * mscale * mscale

F32 = jnp.float32
BF16 = jnp.bfloat16
NT = (((1,), (1,)), ((), ()))
TN = (((0,), (0,)), ((), ()))
NN = (((1,), (0,)), ((), ()))


def dot(a, b, dims):
    return lax.dot_general(a, b, dims, preferred_element_type=F32)


def freqs_of(width):
    half_width = width // 2
    index = np.arange(half_width, dtype=np.float64)
    extrapolated = rope_base ** (-2.0 * index / width)
    span = 2.0 * math.log(rope_base)
    lowest = max(math.floor(width * math.log(pretrain_context / (64.0 * math.pi)) / span), 0)
    highest = min(math.ceil(width * math.log(pretrain_context / (2.0 * math.pi)) / span), width - 1)
    ramp = np.clip((index - lowest) / (highest - lowest), 0.0, 1.0)
    return (extrapolated / yarn_factor * ramp + extrapolated * (1.0 - ramp)).astype(np.float32)


def lane_of(rows):
    return lax.broadcasted_iota(jnp.int32, (rows, LANES), 1)


def swap_halves(m):
    lane = lane_of(m.shape[0])
    return jnp.where((lane & 32) == 0, pltpu.roll(m, 96, 1), pltpu.roll(m, 32, 1))


def fill_tables(first, pos, freq, cos, sin):
    p = pos[0:1, pl.ds(pl.multiple_of(first, 128), 128)].astype(F32)
    angles = jnp.broadcast_to(p, (128, 128)).T * freq[0:1, :]
    span = pl.ds(first, 128)
    cos[span, :] = jnp.cos(angles)
    s = jnp.sin(angles)
    sin[span, :] = jnp.where((lane_of(128) & 32) == 0, -s, s)


def project_rows(first, rows, lat, key_up, value_up, kslot, krot, values):
    span = pl.ds(first, rows)
    low = lane_of(rows) < 64
    compressed = lat[span, :D_C]
    both = lat[span, D_C:].astype(F32)
    krot[span, :] = jnp.where(low, both, 0.0).astype(BF16)

    def pair(p, _):
        source = pl.ds(pl.multiple_of(p * 256, 256), 256)
        keys = dot(compressed, key_up[:, source], NN)
        values[span, source] = dot(compressed, value_up[:, source], NN).astype(BF16)
        turned = pltpu.roll(keys[:, 128:], 64, 1)
        kslot[span, pl.ds(pl.multiple_of(p * 384, 128), 128)] = keys[:, :128].astype(BF16)
        kslot[span, pl.ds(pl.multiple_of(p * 384 + 128, 128), 128)] = jnp.where(low, 0.0, turned).astype(BF16)
        kslot[span, pl.ds(pl.multiple_of(p * 384 + 256, 128), 128)] = jnp.where(low, turned, both).astype(BF16)
        return 0

    lax.fori_loop(0, key_up.shape[1] // 256, pair, 0)


def turn_queries(first, rows, pairs, qbuf, cos, sin):
    span = pl.ds(first, rows)
    low = lane_of(rows) < 64
    c, s = cos[span, :], sin[span, :]

    def pair(p, _):
        at1 = pl.ds(pl.multiple_of(p * 384 + 128, 128), 128)
        at2 = pl.ds(pl.multiple_of(p * 384 + 256, 128), 128)
        one, two = qbuf[span, at1].astype(F32), qbuf[span, at2].astype(F32)
        m = jnp.where(low, one, two)
        r = m * c + swap_halves(m) * s
        qbuf[span, at1] = jnp.where(low, r, one).astype(BF16)
        qbuf[span, at2] = jnp.where(low, two, r).astype(BF16)
        return 0

    lax.fori_loop(*pairs, pair, 0)


def fill_bias(first, pos, bias):
    for half in range(2):
        p = pos[0:1, pl.ds(pl.multiple_of(first + half * 128, 128), 128)]
        c = lax.broadcasted_iota(jnp.int32, (384, 128), 0)
        r = lax.broadcasted_iota(jnp.int32, (384, 128), 1) + 256
        seen = (c <= r) & (c >= r - p)
        bias[half] = jnp.where(seen, 0.0, BIG)


def weigh(scores, dprob, bias):
    probs, grads = [], []
    for half in range(2):
        rows, cols = slice(128 * half, 128 * half + 384), slice(128 * half, 128 * half + 128)
        s = scores[rows, cols] + bias[half]
        d = dprob[rows, cols]
        top = jnp.max(s, axis=0, keepdims=True)
        e = jnp.exp2((s - top) * (SCALING * math.log2(math.e)))
        total = jnp.sum(e, axis=0, keepdims=True)
        share = 1.0 / total
        delta = jnp.sum(e * d, axis=0, keepdims=True) * share
        prob = e * share
        grad = (prob * ((d - delta) * SCALING)).astype(BF16)
        prob = prob.astype(BF16)
        none = jnp.zeros((128, 128), BF16)
        order = (lambda x: [x, none]) if half == 0 else (lambda x: [none, x])
        probs.append(jnp.concatenate(order(prob), axis=0))
        grads.append(jnp.concatenate(order(grad), axis=0))
    return jnp.concatenate(probs, axis=1), jnp.concatenate(grads, axis=1)


def attend(first, pairs, qbuf, gout, kslot, krot, values, bias, cos, sin, dq, dkacc, dvacc):
    qs, ks = pl.ds(first, 256), pl.ds(first, 512)

    def pair(p, _):
        s0 = pl.multiple_of(p * 384, 128)
        v0 = pl.multiple_of(p * 256, 256)
        q = qbuf[qs, pl.ds(s0, 384)]
        g = gout[qs, pl.ds(v0, 256)]
        k0 = jnp.concatenate([kslot[ks, pl.ds(s0, 128)], krot[ks, :]], axis=1)
        k1 = kslot[ks, pl.ds(pl.multiple_of(s0 + 128, 128), 256)]
        dqs, dks = [], []
        for odd, k in ((0, k0), (1, k1)):
            qh = q[:, 128 * odd : 128 * odd + 256]
            gh = g[:, 128 * odd : 128 * odd + 128]
            vh = values[ks, pl.ds(pl.multiple_of(v0 + 128 * odd, 128), 128)]
            scores = dot(k, qh, NT)
            dprob = dot(vh, gh, NT)
            prob, grad = weigh(scores, dprob, bias)
            dvacc[ks, pl.ds(pl.multiple_of(v0 + 128 * odd, 128), 128)] += dot(prob, gh, NN)
            dks.append(dot(grad, qh, NN))
            dqs.append(dot(grad, k, TN))
        low = lane_of(512) < 64
        dkacc[ks, pl.ds(s0, 128)] += dks[0][:, :128]
        dkacc[ks, pl.ds(pl.multiple_of(s0 + 128, 128), 128)] += jnp.where(low, dks[0][:, 128:], dks[1][:, :128])
        dkacc[ks, pl.ds(pl.multiple_of(s0 + 256, 128), 128)] += dks[1][:, 128:]
        low = lane_of(256) < 64
        one, two = dqs[0][:, 128:] + dqs[1][:, :128], dqs[1][:, 128:]
        m = jnp.where(low, one, two)
        r = m * cos[qs, :] - swap_halves(m) * sin[qs, :]
        dq[qs, pl.ds(s0, 128)] = dqs[0][:, :128].astype(BF16)
        dq[qs, pl.ds(pl.multiple_of(s0 + 128, 128), 128)] = jnp.where(low, r, one).astype(BF16)
        dq[qs, pl.ds(pl.multiple_of(s0 + 256, 128), 128)] = jnp.where(low, two, r).astype(BF16)
        return 0

    lax.fori_loop(*pairs, pair, 0, unroll=2)


def gather_back(first, rows, key_up, value_up, dkacc, dvacc):
    span = pl.ds(first, rows)
    low = lane_of(rows) < 64
    total = jnp.zeros((rows, D_C), F32)
    turn = jnp.zeros((rows, LANES), F32)
    for p in range(key_up.shape[1] // 256):
        one = dkacc[span, 384 * p + 128 : 384 * p + 256]
        two = dkacc[span, 384 * p + 256 : 384 * p + 384]
        turn = turn + jnp.where(low, one, two)
        odd = pltpu.roll(jnp.where(low, two, one), 64, 1).astype(BF16)
        even = dkacc[span, 384 * p : 384 * p + 128].astype(BF16)
        cols = slice(256 * p, 256 * p + 256)
        total = total + dot(jnp.concatenate([even, odd], axis=1), key_up[:, cols], NT)
        total = total + dot(dvacc[span, cols].astype(BF16), value_up[:, cols], NT)
    return total, turn + pltpu.roll(turn, 64, 1)


STEPS = ((0, 1), (1, 0), (1, 1), (3, 0), (3, 1), (2, 0), (2, 1))


def kernel(
    query, gout_hbm, lat_in, pos, key_hbm, value_hbm, freq, dq_hbm, glat,
    qbuf, lat, gout, key_up, value_up, cos, sin, kslot, krot, values, bias, dkacc, dvacc, dq, sbuf, own, rbuf, hbuf,
    load_sem, store_sem, lat_send, lat_recv, q_send, q_recv, g_send, g_recv, h_send, h_recv,
):
    g, b = lax.axis_index("grp"), lax.axis_index("blk")
    nb = lax.axis_size("blk")
    z, y = g // 2, g % 2
    slots = qbuf.shape[1]
    group_tok = qbuf.shape[0]
    ahead, behind = (b + 1) % nb, (b + nb - 1) % nb

    def peer(step):
        return ((z + step[0]) % 4) * 2 + (y + step[1]) % 2

    def remote(src, dst, send, recv, to_g=None, to_b=None):
        return pltpu.make_async_remote_copy(
            src_ref=src,
            dst_ref=dst,
            send_sem=send,
            recv_sem=recv,
            device_id=(g if to_g is None else to_g, b if to_b is None else to_b),
            device_id_type=pl.DeviceIdType.MESH,
        )

    loads = [
        pltpu.make_async_copy(key_hbm, key_up, load_sem.at[0]),
        pltpu.make_async_copy(value_hbm, value_up, load_sem.at[1]),
        pltpu.make_async_copy(
            query.at[:, pl.ds(pl.multiple_of(g * slots, 128), slots)],
            qbuf.at[pl.ds(pl.multiple_of(g * 128, 128), 128), :],
            load_sem.at[2],
        ),
        pltpu.make_async_copy(gout_hbm, gout, load_sem.at[3]),
    ]

    barrier = pltpu.get_barrier_semaphore()
    for step in STEPS:
        pl.semaphore_signal(barrier, inc=1, device_id=(peer(step), b), device_id_type=pl.DeviceIdType.MESH)
    for other in (ahead, behind):
        pl.semaphore_signal(barrier, inc=1, device_id=(g, other), device_id_type=pl.DeviceIdType.MESH)

    my = pl.multiple_of(g * 128, 128)
    mine = pl.ds(my, 128)
    fill_tables(my, pos, freq, cos, sin)

    def rows_of(gg):
        return pl.ds(pl.multiple_of(256 + gg * 128, 128), 128)

    raw = lat_in[D_C:, :].astype(F32)
    raw = jnp.concatenate([raw, raw], axis=0).T
    turned = (raw * cos[mine, :] + swap_halves(raw) * sin[mine, :]).astype(BF16)
    lat[rows_of(g), :D_C] = lat_in[:D_C, :].astype(F32).T.astype(BF16)
    lat[rows_of(g), D_C:] = turned

    pl.semaphore_wait(barrier, 9)

    def lat_copy(i, of_g, to_g):
        return remote(lat.at[rows_of(of_g), :], lat.at[rows_of(of_g), :], lat_send.at[i], lat_recv.at[i], to_g=to_g)

    mate = z * 2 + 1 - y
    first_copies = [lat_copy(0, g, mate)] + [
        lat_copy(1 + i, g, peer((dz, 0))) for i, dz in enumerate((1, 3, 2))
    ]
    for copy in first_copies:
        copy.start()
    half = slots // 2
    q_copies = {}
    for dz, dy in STEPS:
        for part in (0, 1) if dz == 2 else (None,):
            n = len(q_copies)
            begin, count = (0, slots) if part is None else (part * half, half)
            q_copies[(dz, dy, part)] = remote(
                query.at[:, pl.ds(pl.multiple_of(peer((dz, dy)) * slots + begin, 128), count)],
                qbuf.at[mine, begin : begin + count],
                q_send.at[n],
                q_recv.at[n],
                to_g=peer((dz, dy)),
            )
    q_copies[(0, 1, None)].start()
    for load in loads:
        load.start()
    first_copies[0].wait_recv()
    second_copies = [lat_copy(4 + i, mate, peer((dz, 0))) for i, dz in enumerate((1, 3, 2))]
    for copy in second_copies:
        copy.start()
    lat_copies = first_copies + second_copies

    dkacc[...] = jnp.zeros_like(dkacc)
    dvacc[...] = jnp.zeros_like(dvacc)

    def table(t, _):
        fill_tables(pl.multiple_of(t * 128, 128), pos, freq, cos, sin)
        return 0

    lax.fori_loop(0, group_tok // 128, table, 0)

    for copy in lat_copies:
        copy.wait_send()
    for copy in lat_copies[1:]:
        copy.wait_recv()
    halo = remote(lat.at[pl.ds(group_tok, 256), :], lat.at[pl.ds(0, 256), :], h_send.at[0], h_recv.at[0], to_b=ahead)
    halo.start()
    for step in ((1, 0), (3, 0), (1, 1), (3, 1)):
        q_copies[(*step, None)].start()
    loads[0].wait()
    loads[1].wait()

    project_rows(256, group_tok, lat, key_up, value_up, kslot, krot, values)
    loads[2].wait()
    loads[3].wait()
    halo.wait_recv()
    project_rows(0, 256, lat, key_up, value_up, kslot, krot, values)

    back = remote(sbuf.at[0:256, :], hbuf, h_send.at[1], h_recv.at[1], to_b=behind)
    g_copies = []

    def return_halo():
        total, turn = gather_back(0, 256, key_up, value_up, dkacc, dvacc)
        sbuf[0:256, :D_C] = total.astype(BF16)
        sbuf[0:256, D_C:] = turn.astype(BF16)
        back.start()

    def send_back(way):
        block = (z + way) % 4
        first = pl.multiple_of(256 + block * 256, 256)
        total, turn = gather_back(first, 256, key_up, value_up, dkacc, dvacc)
        if way:
            sbuf[pl.ds(first, 256), :D_C] = total.astype(BF16)
            sbuf[pl.ds(first, 256), D_C:] = turn.astype(BF16)
        else:
            own[:, :D_C] = total
            own[:, D_C:] = turn

        @pl.when(block == 3)
        def _():
            back.wait_recv()
            if way:
                sbuf[pl.ds(first, 256), :] = (sbuf[pl.ds(first, 256), :].astype(F32) + hbuf[...].astype(F32)).astype(BF16)
            else:
                own[...] += hbuf[...].astype(F32)

        if not way:
            row = pl.multiple_of((1 - y) * 128, 128)
            sbuf[pl.ds(pl.multiple_of(first + row, 128), 128), :] = own[pl.ds(row, 128), :].astype(BF16)
        for i, step in enumerate(STEPS):
            if step[0] == way:
                copy = remote(sbuf.at[rows_of(peer(step)), :], rbuf.at[i], g_send.at[i], g_recv.at[i], to_g=peer(step))
                copy.start()
                g_copies.append(copy)

    def send_back_far():
        for i, step in enumerate(STEPS):
            if step[0] != 2:
                continue
            to = peer(step)
            span = rows_of(to)
            total, turn = gather_back(pl.multiple_of(256 + to * 128, 128), 128, key_up, value_up, dkacc, dvacc)
            sbuf[span, :D_C] = total.astype(BF16)
            sbuf[span, D_C:] = turn.astype(BF16)

            @pl.when(to // 2 == 3)
            def _():
                if step[1] == 0:
                    back.wait_recv()
                part = hbuf[pl.ds(pl.multiple_of((to % 2) * 128, 128), 128), :].astype(F32)
                sbuf[span, :] = (sbuf[span, :].astype(F32) + part).astype(BF16)

            copy = remote(sbuf.at[span, :], rbuf.at[i], g_send.at[i], g_recv.at[i], to_g=to)
            copy.start()
            g_copies.append(copy)

    stores = []
    for i, way in enumerate((0, 3, 1, 2)):
        block = (z + way) % 4
        first = pl.multiple_of(block * 256, 256)
        for part in (0, 1) if way == 2 else (None,):
            for dy in (0, 1):
                if way or dy:
                    q_copies[((4 - way) % 4, dy, part)].wait_recv()
            pairs = (0, slots // 384) if part is None else (part * slots // 768, (part + 1) * slots // 768)
            turn_queries(first, 256, pairs, qbuf, cos, sin)
            if not part:
                fill_bias(first, pos, bias)
            attend(first, pairs, qbuf, gout, kslot, krot, values, bias, cos, sin, dq, dkacc, dvacc)
        store = pltpu.make_async_copy(dq.at[pl.ds(first, 256), :], dq_hbm.at[pl.ds(first, 256), :], store_sem.at[i])
        store.start()
        stores.append(store)
        if i == 0:
            for part in (0, 1):
                q_copies[(2, 0, part)].start()
                q_copies[(2, 1, part)].start()
        if i < 3:
            pl.when(block == 0)(return_halo)
        if i == 1:
            send_back(3)
        if i == 2:
            send_back(0)
        if i == 3:
            send_back_far()
            pl.when(block == 0)(return_halo)
            send_back(1)

    total = own[pl.ds(pl.multiple_of(y * 128, 128), 128), :]
    for copy in g_copies:
        copy.wait_recv()
    for i in range(len(STEPS)):
        total = total + rbuf[i].astype(F32)
    turn = total[:, D_C:]
    turn = turn * cos[mine, :] - swap_halves(turn) * sin[mine, :]
    glat[:D_C, :] = total[:, :D_C].T.astype(BF16)
    glat[D_C:, :] = turn.T[:D_R, :].astype(BF16)

    for copy in list(q_copies.values()) + g_copies + [halo, back]:
        copy.wait_send()
    for store in stores:
        store.wait()


def per_device(query, latent, positions, key_up, value_up, grad_out):
    tok_dev = query.shape[1]
    group_tok = tok_dev * lax.axis_size("grp")
    key_rows = 256 + group_tok
    slots = query.shape[2] // lax.axis_size("grp")
    width = key_up.shape[1]
    wide = D_C + LANES
    freq = jnp.asarray(np.tile(freqs_of(D_R), 4)[None])
    hbm, vmem = pl.BlockSpec(memory_space=pl.ANY), pl.BlockSpec(memory_space=pltpu.VMEM)
    dma = pltpu.SemaphoreType.DMA
    grad_query, grad_latent = pl.pallas_call(
        kernel,
        out_shape=(
            jax.ShapeDtypeStruct((group_tok, slots), BF16),
            jax.ShapeDtypeStruct((D_C + D_R, tok_dev), BF16),
        ),
        in_specs=[hbm, hbm, vmem, vmem, hbm, hbm, vmem],
        out_specs=(hbm, vmem),
        scratch_shapes=[
            pltpu.VMEM((group_tok, slots), BF16),
            pltpu.VMEM((key_rows, wide), BF16),
            pltpu.VMEM((group_tok, width), BF16),
            pltpu.VMEM((D_C, width), BF16),
            pltpu.VMEM((D_C, width), BF16),
            pltpu.VMEM((group_tok, LANES), F32),
            pltpu.VMEM((group_tok, LANES), F32),
            pltpu.VMEM((key_rows, slots), BF16),
            pltpu.VMEM((key_rows, LANES), BF16),
            pltpu.VMEM((key_rows, width), BF16),
            pltpu.VMEM((2, 384, 128), F32),
            pltpu.VMEM((key_rows, slots), F32),
            pltpu.VMEM((key_rows, width), F32),
            pltpu.VMEM((group_tok, slots), BF16),
            pltpu.VMEM((key_rows, wide), BF16),
            pltpu.VMEM((256, wide), F32),
            pltpu.VMEM((7, tok_dev, wide), BF16),
            pltpu.VMEM((256, wide), BF16),
            dma((4,)),
            dma((4,)),
            dma((7,)),
            dma((7,)),
            dma((9,)),
            dma((9,)),
            dma((7,)),
            dma((7,)),
            dma((2,)),
            dma((2,)),
        ],
        compiler_params=pltpu.CompilerParams(
            vmem_limit_bytes=60 * 1024 * 1024, collective_id=0, has_side_effects=True
        ),
    )(query[0], grad_out[0], latent[0].T, positions, key_up, value_up, freq)
    return (grad_query[None], grad_latent.T[None])


def solution(mesh):
    placed = (
        P("blk", "grp", None),
        P("blk", "grp", None),
        P("blk", None),
        P(None, "grp"),
        P(None, "grp"),
        P("blk", None, "grp"),
    )
    return jax.shard_map(
        per_device,
        mesh=mesh,
        in_specs=placed,
        out_specs=(P("blk", None, "grp"), P("blk", "grp", None)),
        check_vma=False,
    )
```
